32 devices in a mesh: cal: 8 (over z, y), gr: 4 (over x, core).
Axes of the slice: x: 2, y: 2, z: 4, core: 2. Of those that a mesh axis runs over, the one named last changes fastest.
Arguments:
- features: bfloat16 [16384, 4096], P('cal', 'gr'), may hold values from -6 to 6
- coef: bfloat16 [4096], P('gr'), may hold values from -0.09375 to 0.09375
- log_exposure: float32 [16384], P('cal'), may hold values from -0.7 to 0.7
- claims: float32 [16384], P('cal'), may hold values from 0 to 4
- cluster_id: int32 [16384], P('cal'), may hold values from 0 to 127
- period: int32 [16384], P('cal'), may hold values from 0 to 15, as said below
- period_effect: float32 [16], replicated, may hold values from -0.5 to 0.5
Outputs:
- meat: float32 [4096, 4096], P('cal', 'gr')
The draws below stay inside these ranges and needn't reach their ends.
Inputs may be any that keep to these rules, and one draw needn't show every extreme that they name: `period`: rows of index d of cal lie in periods d * 2 to (d + 1) * 2 - 1.
All inputs are finite; a program needn't handle non-finite values.
Results may differ from the reference program's by a relative error of at most 0.0044.
Values sent between devices are 32-bit elements; how exact they have to be, the bound alone decides.
No kernel may reach another device: no remote copies, remote signals or barrier semaphores. Data moves between devices by JAX's collectives and lax.ppermute only.
A program may use at most 64 MiB of HBM per device.

```python
import math
import jax
import jax.numpy as jnp
import numpy as np
from jax import lax

P_SIZE = 4096
ROWS_DEV = 2048
PER_DEV = 2
ROWS = 16384
CLUSTERS = 128
PERIODS = 16


def draw_period(key, part):
    base = jnp.arange(ROWS, dtype=jnp.int32) // ROWS_DEV * PER_DEV
    extra = jax.random.randint(key, (ROWS,), 0, PER_DEV, dtype=jnp.int32)
    return (base + extra).astype(jnp.int32)


def touch_ends(entries, own_key, least, largest):
    longest = entries.shape.index(max(entries.shape))
    spots = []
    for shift in (0, 1):
        where = [jax.random.randint(jax.random.fold_in(own_key, axis), (), 0, length) for axis, length in enumerate(entries.shape)]
        where[longest] = (where[longest] + shift) % entries.shape[longest]
        spots.append(tuple(where))
    return entries.at[spots[0]].set(least).at[spots[1]].set(largest)


def levels(key, shape, pieces, least, high):
    def one(dim, blocks):
        steps = jax.random.uniform(jax.random.fold_in(jax.random.fold_in(key, 6), dim), (blocks,), jnp.float32, least / len(pieces), high / len(pieces))
        return jnp.repeat(jnp.exp(steps), shape[dim] // blocks).reshape((-1,) + (1,) * (len(shape) - dim - 1))

    loudness = one(*pieces[0])
    for cut in pieces[1:]:
        loudness = loudness * one(*cut)
    return loudness


def rank_bounds(amount, slope):
    loads = [(1 << 20) // math.isqrt(standing ** slope) + 1 for standing in range(1, amount + 1)]
    spread = 1 + sum(loads) // (1 << 30)
    return np.cumsum(np.array([max(1, weight // spread) for weight in loads]))


def skewed_ids(stream_key, extent, amount, skew):
    grid = rank_bounds(amount, skew)
    ticket = jax.random.randint(jax.random.fold_in(stream_key, 1), extent, 0, int(grid[amount - 1]))
    rank = jnp.searchsorted(jnp.asarray(grid, jnp.int32), ticket, side="right")
    return jax.random.permutation(jax.random.fold_in(stream_key, 2), amount)[rank].astype(jnp.int32)


def normal_values(own_key, shape, spread, limit, pieces=(), held_as=jnp.bfloat16):
    values = spread * jax.random.normal(own_key, shape, jnp.float32)
    if pieces:
        values = values * levels(own_key, shape, pieces, -0.22, 0.18)
    return jnp.clip(values, -limit, limit).astype(held_as)


def setup_inputs(seed: int = 0) -> dict:
    key_of = jax.random.split(jax.random.key(seed), 8)
    features = normal_values(key_of[0], (ROWS, P_SIZE), 1.0, 6.0, ((0, 8), (1, 4)))
    coef = normal_values(key_of[1], (P_SIZE,), P_SIZE ** -0.5, 0.09375, ((0, 4),))
    log_exposure = jnp.clip(jax.random.uniform(key_of[2], (ROWS,), jnp.float32, -0.7, 0.7) * levels(key_of[2], (ROWS,), ((0, 8),), -0.4, 0.0), -0.7, 0.7)
    claims = jnp.clip(4.0 * jax.random.uniform(key_of[3], (ROWS,), jnp.float32) ** levels(key_of[3], (ROWS,), ((0, 8),), -0.2, 0.2), 0.0, 4.0)
    cluster_id = touch_ends(skewed_ids(key_of[4], (ROWS,), CLUSTERS, 1), jax.random.fold_in(key_of[4], 3), 0, CLUSTERS - 1).astype(jnp.int32)
    period = draw_period(jax.random.fold_in(key_of[7], 71), 0)
    period_effect = jnp.clip(jax.random.uniform(key_of[6], (PERIODS,), jnp.float32, -0.5, 0.5), -0.5, 0.5)
    return dict(features=features, coef=coef, log_exposure=log_exposure, claims=claims, cluster_id=cluster_id, period=period, period_effect=period_effect)


def reference(features, coef, log_exposure, claims, cluster_id, period, period_effect):
    linear = jnp.dot(features, coef, preferred_element_type=jnp.float32)
    table = jnp.where(period[:, None] == jnp.arange(PERIODS, dtype=jnp.int32)[None, :], period_effect[None, :], jnp.float32(0.0))
    shift = jnp.sum(table, axis=1)
    resid = (claims - jnp.exp(linear + log_exposure + shift)).astype(jnp.bfloat16)
    block = ROWS_DEV
    count = ROWS // block
    feats = features.reshape(count, block, P_SIZE)
    res_b = resid.reshape(count, block)
    ids_b = cluster_id.reshape(count, block)

    def step(carry, item):
        feat_blk, res_blk, id_blk = item
        weighted = feat_blk.astype(jnp.float32) * res_blk.astype(jnp.float32)[:, None]
        return carry + jax.ops.segment_sum(weighted, id_blk, num_segments=CLUSTERS), None

    score, _ = lax.scan(step, jnp.zeros((CLUSTERS, P_SIZE), jnp.float32), (feats, res_b, ids_b))
    meat = jnp.dot(score.T, score, precision=lax.Precision.HIGHEST, preferred_element_type=jnp.float32)
    return meat / jnp.float32(ROWS)
```

```python
import functools

import jax
import jax.numpy as jnp
from jax import lax
from jax.experimental import pallas as pl
from jax.experimental.pallas import tpu as pltpu
from jax.sharding import PartitionSpec as P

CL_DEV = 16
AXES = ("cal", "gr")
VMEM = pl.BlockSpec(memory_space=pltpu.VMEM)
SMEM = pl.BlockSpec(memory_space=pltpu.SMEM)
ANY = pl.BlockSpec(memory_space=pl.ANY)
LIMIT = 40 * 1024 * 1024


def split_two(value):
    high = value.astype(jnp.bfloat16)
    low = (value - high.astype(jnp.float32)).astype(jnp.bfloat16)
    return high, low


def linear_kernel(pieces, feats, coef, lin, held, sems):
    rows = held.shape[0] // pieces
    copies = []
    for i in range(pieces):
        part = pl.ds(i * rows, rows)
        copies.append(pltpu.make_async_copy(feats.at[part], held.at[part], sems.at[i]))
        copies[-1].start()
    weights = jnp.broadcast_to(coef[...], (16, coef.shape[1]))
    for i in range(pieces):
        copies[i].wait()
        out = lax.dot_general(
            weights,
            held[i * rows : (i + 1) * rows, :],
            (((1,), (1,)), ((), ())),
            preferred_element_type=jnp.float32,
        )
        lin[:, i * rows : (i + 1) * rows] = out[0:1]


def linear_call(features, coef):
    rows, width = features.shape
    pieces = 8
    return pl.pallas_call(
        functools.partial(linear_kernel, pieces),
        out_shape=(
            jax.ShapeDtypeStruct((1, rows), jnp.float32),
            jax.ShapeDtypeStruct((rows, width), features.dtype),
        ),
        in_specs=[ANY, VMEM],
        out_specs=(VMEM, VMEM),
        scratch_shapes=[pltpu.SemaphoreType.DMA((pieces,))],
        compiler_params=pltpu.CompilerParams(vmem_limit_bytes=LIMIT),
        cost_estimate=pl.CostEstimate(
            flops=2 * rows * width, bytes_accessed=2 * rows * width, transcendentals=0
        ),
        name="linear",
    )(features, coef)


def picks_kernel(first, where, effect, lin_a, lin_b, exposure, claims, ids, period, held, out, picks):
    base = where[0]
    shift = jnp.zeros(lin_a.shape, jnp.float32)
    for k in range(first):
        shift = jnp.where(period[...] == base + k, effect[base + k], shift)
    linear = lin_a[...] + lin_b[...]
    resid = claims[...] - jnp.exp(linear + exposure[...] + shift)
    clusters, rows = picks.shape
    resid = resid.astype(jnp.bfloat16).astype(jnp.float32)
    cluster = lax.broadcasted_iota(jnp.int32, (clusters, rows), 0)
    picks[...] = jnp.where(cluster == ids[...], resid, 0.0).astype(jnp.bfloat16)
    half = out.shape[1]
    columns = pl.ds(pl.multiple_of(where[1] * half, half), half)
    out[...] = jnp.dot(picks[...], held[:, columns], preferred_element_type=jnp.float32)


def keep_kernel(where, picks, held, out):
    half = out.shape[1]
    columns = pl.ds(pl.multiple_of(where[0] * half, half), half)
    out[...] = jnp.dot(picks[...], held[:, columns], preferred_element_type=jnp.float32)


def meat_kernel(scale, where, own_rows, near_rows, far_rows, own, other, out):
    mode = where[0]
    rows = jnp.where(mode == 0, own_rows[...], jnp.where(mode == 1, near_rows[...], far_rows[...]))
    left_high, left_low = split_two(rows)
    left = jnp.concatenate([left_high, left_low], axis=0)
    half = own.shape[1]
    for k, part in enumerate((own, other)):
        high, low = split_two(part[...])
        dims = (((0,), (0,)), ((), ()))
        total = lax.dot_general(
            left, jnp.concatenate([high, high], axis=0), dims, preferred_element_type=jnp.float32
        ) + lax.dot_general(left_high, low, dims, preferred_element_type=jnp.float32)
        spot = where[1] if k == 0 else 1 - where[1]
        out[:, pl.ds(pl.multiple_of(spot * half, half), half)] = total * scale


def exchange(value, cal_bits, gr_bits, n_cal, n_gr):
    pairs = [
        (c * n_gr + g, (c ^ cal_bits) * n_gr + (g ^ gr_bits))
        for c in range(n_cal)
        for g in range(n_gr)
    ]
    return lax.ppermute(value, AXES, pairs)


def per_device(features, coef, log_exposure, claims, cluster_id, period, period_effect):
    rows, width = features.shape
    n_cal, n_gr = lax.axis_size("cal"), lax.axis_size("gr")
    clusters = CL_DEV * n_cal
    per_dev = period_effect.shape[0] // n_cal
    fan = n_cal // n_gr
    cal, gr = lax.axis_index("cal"), lax.axis_index("gr")
    high, low = cal // fan, cal % fan
    swap = functools.partial(exchange, n_cal=n_cal, n_gr=n_gr)

    lin, held = linear_call(features, coef.reshape(1, width))
    bits = 1
    while bits < n_gr // 2:
        lin = lin + swap(lin, 0, bits)
        bits *= 2
    lin_far = swap(lin, 0, bits)

    half = width // 2
    top = low // (fan // 2)
    flat = [v.reshape(1, rows) for v in (log_exposure, claims, cluster_id, period)]
    send, picks = pl.pallas_call(
        functools.partial(picks_kernel, per_dev),
        out_shape=(
            jax.ShapeDtypeStruct((clusters, half), jnp.float32),
            jax.ShapeDtypeStruct((clusters, rows), jnp.bfloat16),
        ),
        in_specs=[SMEM, SMEM] + [VMEM] * 7,
        out_specs=(VMEM, VMEM),
        compiler_params=pltpu.CompilerParams(vmem_limit_bytes=LIMIT),
        cost_estimate=pl.CostEstimate(
            flops=2 * rows * clusters * half, bytes_accessed=rows * width, transcendentals=rows
        ),
        name="send_half",
    )(
        jnp.stack([cal * per_dev, 1 - top]).astype(jnp.int32),
        period_effect, lin, lin_far, *flat, held,
    )
    there = swap(send, fan // 2, 0)
    keep = pl.pallas_call(
        keep_kernel,
        out_shape=jax.ShapeDtypeStruct((clusters, half), jnp.float32),
        in_specs=[SMEM, VMEM, VMEM],
        out_specs=VMEM,
        compiler_params=pltpu.CompilerParams(vmem_limit_bytes=LIMIT),
        cost_estimate=pl.CostEstimate(
            flops=2 * rows * clusters * half, bytes_accessed=rows * width, transcendentals=0
        ),
        name="keep_half",
    )(top.astype(jnp.int32).reshape(1), picks, held)
    part = keep + there
    bits = fan // 4
    while bits:
        size = part.shape[1] // 2
        mine = (low // bits) % 2
        away = lax.dynamic_slice_in_dim(part, (1 - mine) * size, size, axis=1)
        part = lax.dynamic_slice_in_dim(part, mine * size, size, axis=1) + swap(away, bits, 0)
        bits //= 2

    group = clusters // n_gr
    owned = lax.dynamic_slice_in_dim(part, high * group, group, axis=0)
    arrived = []
    for k in range(n_gr - 1, 0, -1):
        piece = lax.dynamic_slice_in_dim(part, (high ^ k) * group, group, axis=0)
        arrived.append(swap(piece, k * fan, 0))
    for piece in arrived:
        owned = owned + piece
    gathered = [swap(owned, k * fan, 0) for k in range(n_gr - 1, 0, -1)]
    block = jnp.concatenate([owned] + gathered[::-1], axis=0)

    side = block
    bits = 1
    while bits < fan // 2:
        mine = (low // bits) % 2
        away = swap(side, bits, 0)
        side = jnp.where(
            mine == 0, jnp.concatenate([side, away], axis=1), jnp.concatenate([away, side], axis=1)
        )
        bits *= 2
    other = swap(side, fan // 2, 0)

    turn = gr ^ high
    have = block
    bits = n_gr // 2
    reach = 0
    near = block
    while bits:
        pairs = []
        for c in range(n_cal):
            for g in range(n_gr):
                if ((g ^ (c // fan)) & ~reach) == 0:
                    pairs.append((c * n_gr + g, c * n_gr + (g ^ bits)))
        got = lax.ppermute(have, AXES, pairs)
        reach |= bits
        if bits == 1:
            near, far = have, got
        else:
            have = jnp.where((turn & bits) != 0, got, have)
        bits //= 2
    mode = jnp.where((turn & 1) != 0, 2, 1)
    scale = 1.0 / (rows * n_cal)
    return pl.pallas_call(
        functools.partial(meat_kernel, scale),
        out_shape=jax.ShapeDtypeStruct((block.shape[1], width), jnp.float32),
        in_specs=[SMEM] + [VMEM] * 5,
        out_specs=VMEM,
        compiler_params=pltpu.CompilerParams(vmem_limit_bytes=LIMIT),
        name="meat",
    )(jnp.stack([mode, top]).astype(jnp.int32), block, near, far, side, other)


def solution(mesh):
    placed = (P("cal", "gr"), P("gr"), P("cal"), P("cal"), P("cal"), P("cal"), P())
    return jax.shard_map(
        per_device, mesh=mesh, in_specs=placed, out_specs=P("cal", "gr"), check_vma=False
    )
```

```python
import functools

import jax
import jax.numpy as jnp
from jax import lax
from jax.experimental import pallas as pl
from jax.experimental.pallas import tpu as pltpu
from jax.sharding import PartitionSpec as P

CL_DEV = 16
AXES = ("cal", "gr")
VMEM = pl.BlockSpec(memory_space=pltpu.VMEM)
SMEM = pl.BlockSpec(memory_space=pltpu.SMEM)
LIMIT = 24 * 1024 * 1024


def position():
    fan = lax.axis_size("cal") // lax.axis_size("gr")
    cal, gr = lax.axis_index("cal"), lax.axis_index("gr")
    return cal, cal // fan, cal % fan, gr


def top_half():
    fan = lax.axis_size("cal") // lax.axis_size("gr")
    return position()[2] // (fan // 2)


def split_two(value):
    high = value.astype(jnp.bfloat16)
    low = (value - high.astype(jnp.float32)).astype(jnp.bfloat16)
    return high, low


def linear_kernel(held, coef, lin, out):
    del out
    rows, width = held.shape
    weights = coef[...].reshape(1, width).astype(jnp.float32)
    step = min(512, rows)
    for i in range(0, rows, step):
        total = jnp.zeros((step, 128), jnp.float32)
        for j in range(0, width, 128):
            total = total + held[i : i + step, j : j + 128].astype(jnp.float32) * weights[:, j : j + 128]
        lin[:, i : i + step] = jnp.sum(total.T, axis=0, keepdims=True)


def picks_kernel(per_dev, group, terms, effect, *refs):
    exposure, claims, ids, period, held, far, near, picks = refs[terms:]
    cal, high, _, _ = position()
    base = cal * per_dev
    shift = jnp.zeros(claims.shape, jnp.float32)
    for k in range(per_dev):
        shift = jnp.where(period[...] == base + k, effect[base + k], shift)
    sums = [ref[...] for ref in refs[:terms]]
    while len(sums) > 1:
        sums = [a + b for a, b in zip(sums[::2], sums[1::2])]
    linear = sums[0]
    resid = claims[...] - jnp.exp(linear + exposure[...] + shift)
    resid = resid.astype(jnp.bfloat16).astype(jnp.float32)
    clusters, rows = picks.shape
    for k in range(clusters // group):
        first = (high ^ k) * group
        cluster = lax.broadcasted_iota(jnp.int32, (group, rows), 0) + first
        picks[k * group : (k + 1) * group, :] = jnp.where(cluster == ids[...], resid, 0.0).astype(jnp.bfloat16)
    half, deep = far.shape[1], far.shape[0]
    columns = pl.ds(pl.multiple_of((1 - top_half()) * half, half), half)
    far[...] = jnp.dot(picks[deep:, :], held[:, columns], preferred_element_type=jnp.float32)
    near[...] = jnp.dot(picks[:deep, :], held[:, columns], preferred_element_type=jnp.float32)


def keep_kernel(picks, held, *outs):
    half, group = outs[0].shape[1], outs[0].shape[0]
    columns = pl.ds(pl.multiple_of(top_half() * half, half), half)
    total = jnp.dot(picks[...], held[:, columns], preferred_element_type=jnp.float32)
    for k, out in enumerate(outs):
        out[...] = total[k * group : (k + 1) * group]


def meat_kernel(scale, have, *refs):
    got, own, other, out = refs[:-5], refs[-5:-3], refs[-3:-1], refs[-1]
    _, high, _, gr = position()
    rows = jnp.where((gr ^ high) % 2 == 0, have[...], jnp.concatenate([ref[...] for ref in got], axis=0))
    left_high, left_low = split_two(rows)
    left = jnp.concatenate([left_high, left_low], axis=0)
    half = own[0].shape[1]
    for k, part in enumerate((own, other)):
        high, low = split_two(jnp.concatenate([p[...] for p in part], axis=0))
        dims = (((0,), (0,)), ((), ()))
        total = lax.dot_general(
            left, jnp.concatenate([high, high], axis=0), dims, preferred_element_type=jnp.float32
        ) + lax.dot_general(left_high, low, dims, preferred_element_type=jnp.float32)
        spot = top_half() if k == 0 else 1 - top_half()
        out[:, pl.ds(pl.multiple_of(spot * half, half), half)] = total * scale


def exchange(value, cal_bits, gr_bits, n_cal, n_gr):
    pairs = [
        (c * n_gr + g, (c ^ cal_bits) * n_gr + (g ^ gr_bits))
        for c in range(n_cal)
        for g in range(n_gr)
    ]
    return lax.ppermute(value, AXES, pairs)


def per_device(features, coef, log_exposure, claims, cluster_id, period, period_effect):
    rows, width = features.shape
    n_cal, n_gr = lax.axis_size("cal"), lax.axis_size("gr")
    clusters = CL_DEV * n_cal
    per_dev = period_effect.shape[0] // n_cal
    fan = n_cal // n_gr
    cal, gr = lax.axis_index("cal"), lax.axis_index("gr")
    high, low = cal // fan, cal % fan
    swap = functools.partial(exchange, n_cal=n_cal, n_gr=n_gr)

    def kernel(body, out_shape, args, scalars, name, flops=0, alias={}):
        outs = out_shape if isinstance(out_shape, tuple) else (out_shape,)
        call = pl.pallas_call(
            body,
            out_shape=out_shape,
            in_specs=[SMEM] * scalars + [VMEM] * (len(args) - scalars),
            out_specs=tuple(VMEM for _ in outs) if isinstance(out_shape, tuple) else VMEM,
            compiler_params=pltpu.CompilerParams(vmem_limit_bytes=LIMIT),
            cost_estimate=pl.CostEstimate(flops=flops, bytes_accessed=flops // 256, transcendentals=0),
            name=name,
            input_output_aliases=alias,
        )
        return call(*args)

    f32, bf16 = jnp.float32, jnp.bfloat16
    lin, features = kernel(
        linear_kernel,
        (jax.ShapeDtypeStruct((1, rows), f32), jax.ShapeDtypeStruct((rows, width), bf16)),
        (features, coef), 0, "linear", 2 * rows * width, {0: 1},
    )
    linears = [lin] + [swap(lin, 0, k) for k in range(1, n_gr)]

    half = width // 2
    deep = clusters // 2
    group = clusters // n_gr
    flat = [v.reshape(1, rows) for v in (log_exposure, claims, cluster_id, period)]
    work = 2 * rows * deep * half
    far, near, picks = kernel(
        functools.partial(picks_kernel, per_dev, group, n_gr),
        (
            jax.ShapeDtypeStruct((deep, half), f32),
            jax.ShapeDtypeStruct((deep, half), f32),
            jax.ShapeDtypeStruct((clusters, rows), bf16),
        ),
        (period_effect, *linears, *flat, features),
        1, "send", 2 * work,
    )
    there = [swap(near, fan // 2, 0), swap(far, fan // 2, 0)]
    kept = kernel(
        keep_kernel, tuple(jax.ShapeDtypeStruct((group, half), f32) for _ in range(n_gr)),
        (picks, features), 0, "keep", 2 * work,
    )
    parts = []
    for k in range(n_gr):
        start = k * group % deep
        part = kept[k] + there[k * group // deep][start : start + group]
        bits = fan // 4
        while bits:
            size = part.shape[1] // 2
            mine = (low // bits) % 2
            away = lax.dynamic_slice_in_dim(part, (1 - mine) * size, size, axis=1)
            part = lax.dynamic_slice_in_dim(part, mine * size, size, axis=1) + swap(away, bits, 0)
            bits //= 2
        parts.append(part)

    arrived = [swap(parts[k], k * fan, 0) for k in range(n_gr - 1, 0, -1)]
    owned = parts[0]
    for part in arrived[::-1]:
        owned = owned + part
    gathered = [owned] + [swap(owned, k * fan, 0) for k in range(n_gr - 1, 0, -1)][::-1]
    blocks = [gathered[0], jnp.concatenate(gathered[1:], axis=0)]
    sides, others = [], []
    for side in blocks:
        bits = 1
        while bits < fan // 2:
            mine = (low // bits) % 2
            away = swap(side, bits, 0)
            side = jnp.where(
                mine == 0, jnp.concatenate([side, away], axis=1), jnp.concatenate([away, side], axis=1)
            )
            bits *= 2
        sides.append(side)
        others.append(swap(side, fan // 2, 0))

    have = jnp.concatenate(gathered, axis=0)
    have, others[0] = lax.optimization_barrier((have, others[0]))
    turn = gr ^ high
    bits = n_gr // 2
    while bits > 1:
        pairs = []
        for c in range(n_cal):
            for g in range(n_gr):
                step = (g ^ (c // fan)) & (2 * bits - 1)
                flip = bits if step == 0 or step == 2 * bits - 1 else bits // 2
                pairs.append((c * n_gr + g, c * n_gr + (g ^ flip)))
        if bits > 2:
            pairs = [(c * n_gr + g, c * n_gr + (g ^ bits)) for c in range(n_cal) for g in range(n_gr)]
        got = lax.ppermute(have, AXES, pairs)
        have = jnp.where((turn & bits) != 0, got, have)
        bits //= 2
    got = [swap(have[k * group : (k + 1) * group], 0, 1) for k in range(n_gr)]
    scale = 1.0 / (rows * n_cal)
    return kernel(
        functools.partial(meat_kernel, scale),
        jax.ShapeDtypeStruct((blocks[0].shape[1], width), f32),
        (have, *got, *sides, *others),
        0, "meat", 6 * clusters * width * blocks[0].shape[1],
    )


def solution(mesh):
    placed = (P("cal", "gr"), P("gr"), P("cal"), P("cal"), P("cal"), P("cal"), P())
    return jax.shard_map(
        per_device, mesh=mesh, in_specs=placed, out_specs=P("cal", "gr"), check_vma=False
    )
```

```python
import functools

import jax
import jax.numpy as jnp
from jax import lax
from jax.experimental import pallas as pl
from jax.experimental.pallas import tpu as pltpu
from jax.sharding import PartitionSpec as P

CL_DEV = 16
AXES = ("cal", "gr")
VMEM = pl.BlockSpec(memory_space=pltpu.VMEM)
SMEM = pl.BlockSpec(memory_space=pltpu.SMEM)
ANY = pl.BlockSpec(memory_space=pl.ANY)
LIMIT = 24 * 1024 * 1024


def position():
    fan = lax.axis_size("cal") // lax.axis_size("gr")
    cal, gr = lax.axis_index("cal"), lax.axis_index("gr")
    return cal, cal // fan, cal % fan, gr


def top_half():
    fan = lax.axis_size("cal") // lax.axis_size("gr")
    return position()[2] // (fan // 2)


def split_two(value):
    high = value.astype(jnp.bfloat16)
    low = (value - high.astype(jnp.float32)).astype(jnp.bfloat16)
    return high, low


def linear_kernel(held, coef, lin, out):
    del out
    rows, width = held.shape
    weights = coef[...].reshape(1, width).astype(jnp.float32)
    step = min(512, rows)
    for i in range(0, rows, step):
        total = jnp.zeros((step, 128), jnp.float32)
        for j in range(0, width, 128):
            total = total + held[i : i + step, j : j + 128].astype(jnp.float32) * weights[:, j : j + 128]
        lin[:, i : i + step] = jnp.sum(total.T, axis=0, keepdims=True)


def spread(total, outs):
    size = outs[0].shape[0]
    for k, out in enumerate(outs):
        out[...] = total[k * size : (k + 1) * size]


def picks_kernel(per_dev, group, terms, effect, *refs):
    exposure, claims, ids, period, held, *far, picks = refs[terms:]
    cal, high, _, _ = position()
    base = cal * per_dev
    shift = jnp.zeros(claims.shape, jnp.float32)
    for k in range(per_dev):
        shift = jnp.where(period[...] == base + k, effect[base + k], shift)
    sums = [ref[...] for ref in refs[:terms]]
    while len(sums) > 1:
        sums = [a + b for a, b in zip(sums[::2], sums[1::2])]
    linear = sums[0]
    resid = claims[...] - jnp.exp(linear + exposure[...] + shift)
    resid = resid.astype(jnp.bfloat16).astype(jnp.float32)
    clusters, rows = picks.shape
    for k in range(clusters // group):
        first = (high ^ k) * group
        cluster = lax.broadcasted_iota(jnp.int32, (group, rows), 0) + first
        picks[k * group : (k + 1) * group, :] = jnp.where(cluster == ids[...], resid, 0.0).astype(jnp.bfloat16)
    half, deep = far[0].shape[1], clusters // 2
    columns = pl.ds(pl.multiple_of((1 - top_half()) * half, half), half)
    spread(jnp.dot(picks[deep:, :], held[:, columns], preferred_element_type=jnp.float32), far)


def rest_kernel(picks, held, *outs):
    half, group = outs[0].shape[1], outs[0].shape[0]
    deep = picks.shape[0] // 2
    columns = pl.ds(pl.multiple_of((1 - top_half()) * half, half), half)
    spread(jnp.dot(picks[:deep, :], held[:, columns], preferred_element_type=jnp.float32), outs[: deep // group])
    columns = pl.ds(pl.multiple_of(top_half() * half, half), half)
    spread(jnp.dot(picks[...], held[:, columns], preferred_element_type=jnp.float32), outs[deep // group :])


def meat_columns(scale, left, parts, store):
    high, low = split_two(jnp.concatenate([p[...] for p in parts], axis=0))
    deep = jnp.concatenate([high, high], axis=0)
    left_high = left[: left.shape[0] // 2]
    dims = (((0,), (0,)), ((), ()))
    half = high.shape[1]
    block = min(256, half)
    for n in range(half // block):
        part = slice(n * block, (n + 1) * block)
        total = lax.dot_general(
            left, deep[:, part], dims, preferred_element_type=jnp.float32
        ) + lax.dot_general(left_high, low[:, part], dims, preferred_element_type=jnp.float32)
        store(n, total * scale)


def own_kernel(scale, have, *refs):
    refs, (out, left) = refs[:-2], refs[-2:]
    got, own = refs[:-2], refs[-2:]
    _, high, _, gr = position()
    rows = jnp.where((gr ^ high) % 2 == 0, have[...], jnp.concatenate([ref[...] for ref in got], axis=0))
    both = jnp.concatenate(split_two(rows), axis=0)
    left[...] = both

    def store(n, value):
        out[n] = value

    meat_columns(scale, both, own, store)


def other_kernel(scale, first, left, *refs):
    other, (out, held, sems) = refs[:-3], refs[-3:]
    parts, _, block = held.shape
    copies = []

    def send(source, n, spot):
        columns = pl.ds(pl.multiple_of((spot * parts + n) * block, block), block)
        copies.append(pltpu.make_async_copy(source.at[n], out.at[:, columns], sems.at[len(copies)]))
        copies[-1].start()

    def store(n, value):
        held[n] = value
        send(held, n, 1 - top_half())

    for n in range(parts):
        send(first, n, top_half())
    meat_columns(scale, left[...], other, store)
    for copy in copies:
        copy.wait()


def exchange(value, cal_bits, gr_bits, n_cal, n_gr):
    pairs = [
        (c * n_gr + g, (c ^ cal_bits) * n_gr + (g ^ gr_bits))
        for c in range(n_cal)
        for g in range(n_gr)
    ]
    return lax.ppermute(value, AXES, pairs)


def per_device(features, coef, log_exposure, claims, cluster_id, period, period_effect):
    rows, width = features.shape
    n_cal, n_gr = lax.axis_size("cal"), lax.axis_size("gr")
    clusters = CL_DEV * n_cal
    per_dev = period_effect.shape[0] // n_cal
    fan = n_cal // n_gr
    cal, gr = lax.axis_index("cal"), lax.axis_index("gr")
    high, low = cal // fan, cal % fan
    swap = functools.partial(exchange, n_cal=n_cal, n_gr=n_gr)

    def kernel(body, out_shape, args, scalars, name, flops=0, alias={}):
        outs = out_shape if isinstance(out_shape, tuple) else (out_shape,)
        call = pl.pallas_call(
            body,
            out_shape=out_shape,
            in_specs=[SMEM] * scalars + [VMEM] * (len(args) - scalars),
            out_specs=tuple(VMEM for _ in outs) if isinstance(out_shape, tuple) else VMEM,
            compiler_params=pltpu.CompilerParams(vmem_limit_bytes=LIMIT),
            cost_estimate=pl.CostEstimate(flops=flops, bytes_accessed=flops // 256, transcendentals=0),
            name=name,
            input_output_aliases=alias,
        )
        return call(*args)

    f32, bf16 = jnp.float32, jnp.bfloat16
    lin, features = kernel(
        linear_kernel,
        (jax.ShapeDtypeStruct((1, rows), f32), jax.ShapeDtypeStruct((rows, width), bf16)),
        (features, coef), 0, "linear", 2 * rows * width, {0: 1},
    )
    linears = [lin] + [swap(lin, 0, k) for k in range(n_gr - 1, 0, -1)]

    half = width // 2
    deep = clusters // 2
    group = clusters // n_gr
    flat = [v.reshape(1, rows) for v in (log_exposure, claims, cluster_id, period)]
    work = 2 * rows * deep * half
    score = jax.ShapeDtypeStruct((group, half), f32)
    *far, picks = kernel(
        functools.partial(picks_kernel, per_dev, group, n_gr),
        (score,) * (n_gr // 2) + (jax.ShapeDtypeStruct((clusters, rows), bf16),),
        (period_effect, *linears, *flat, features),
        1, "send_far", work,
    )
    far = [swap(value, fan // 2, 0) for value in far]
    rest = kernel(rest_kernel, (score,) * (n_gr // 2 + n_gr), (picks, features), 0, "rest", 3 * work)
    there = [swap(value, fan // 2, 0) for value in rest[: n_gr // 2]] + far
    kept = rest[n_gr // 2 :]
    parts = []
    for k in range(n_gr):
        part = kept[k] + there[k]
        bits = fan // 4
        while bits:
            size = part.shape[1] // 2
            mine = (low // bits) % 2
            away = lax.dynamic_slice_in_dim(part, (1 - mine) * size, size, axis=1)
            part = lax.dynamic_slice_in_dim(part, mine * size, size, axis=1) + swap(away, bits, 0)
            bits //= 2
        parts.append(part)

    arrived = {k: swap(parts[k], k * fan, 0) for k in range(n_gr - 1, 0, -1)}
    owned = lax.optimization_barrier(arrived[n_gr // 2] + arrived[n_gr // 2 + 1])
    for k in [*range(n_gr // 2 + 2, n_gr), *range(1, n_gr // 2)]:
        owned = owned + arrived[k]
    owned = owned + parts[0]
    gathered = [owned] + [swap(owned, k * fan, 0) for k in range(n_gr - 1, 0, -1)]
    blocks = [gathered[0], jnp.concatenate(gathered[1:], axis=0)]
    sides, others = [], []
    for side in blocks:
        bits = 1
        while bits < fan // 2:
            mine = (low // bits) % 2
            away = swap(side, bits, 0)
            side = jnp.where(
                mine == 0, jnp.concatenate([side, away], axis=1), jnp.concatenate([away, side], axis=1)
            )
            bits *= 2
        sides.append(side)
        others.append(swap(side, fan // 2, 0))

    have = jnp.concatenate(gathered, axis=0)
    have, others[0] = lax.optimization_barrier((have, others[0]))
    turn = gr ^ high
    bits = n_gr // 2
    while bits > 1:
        pairs = []
        for c in range(n_cal):
            for g in range(n_gr):
                step = (g ^ (c // fan)) & (2 * bits - 1)
                flip = bits if step == 0 or step == 2 * bits - 1 else bits // 2
                pairs.append((c * n_gr + g, c * n_gr + (g ^ flip)))
        if bits > 2:
            pairs = [(c * n_gr + g, c * n_gr + (g ^ bits)) for c in range(n_cal) for g in range(n_gr)]
        got = lax.ppermute(have, AXES, pairs)
        have = jnp.where((turn & bits) != 0, got, have)
        bits //= 2
    got = [swap(have[k * group : (k + 1) * group], 0, 1) for k in range(n_gr)]
    scale = 1.0 / (rows * n_cal)
    wide, block = have.shape[1], min(256, half)
    parts = half // block
    work = 6 * clusters * half * wide
    first, left = kernel(
        functools.partial(own_kernel, scale),
        (jax.ShapeDtypeStruct((parts, wide, block), f32), jax.ShapeDtypeStruct((2 * clusters, wide), bf16)),
        (have, *got, *sides), 0, "meat_own", work,
    )
    args = (first, left, *others)
    return pl.pallas_call(
        functools.partial(other_kernel, scale),
        out_shape=jax.ShapeDtypeStruct((wide, width), f32),
        in_specs=[VMEM] * len(args),
        out_specs=ANY,
        scratch_shapes=[pltpu.VMEM((parts, wide, block), f32), pltpu.SemaphoreType.DMA((2 * parts,))],
        compiler_params=pltpu.CompilerParams(vmem_limit_bytes=LIMIT),
        cost_estimate=pl.CostEstimate(flops=work, bytes_accessed=4 * wide * width, transcendentals=0),
        name="meat_other",
    )(*args)


def solution(mesh):
    placed = (P("cal", "gr"), P("gr"), P("cal"), P("cal"), P("cal"), P("cal"), P())
    return jax.shard_map(
        per_device, mesh=mesh, in_specs=placed, out_specs=P("cal", "gr"), check_vma=False
    )
```

```python
import functools

import jax
import jax.numpy as jnp
from jax import lax
from jax.experimental import pallas as pl
from jax.experimental.pallas import tpu as pltpu
from jax.sharding import PartitionSpec as P

CL_DEV = 16
AXES = ("cal", "gr")
VMEM = pl.BlockSpec(memory_space=pltpu.VMEM)
SMEM = pl.BlockSpec(memory_space=pltpu.SMEM)
ANY = pl.BlockSpec(memory_space=pl.ANY)
LIMIT = 24 * 1024 * 1024


def position():
    fan = lax.axis_size("cal") // lax.axis_size("gr")
    cal, gr = lax.axis_index("cal"), lax.axis_index("gr")
    return cal, cal // fan, cal % fan, gr


def top_half():
    fan = lax.axis_size("cal") // lax.axis_size("gr")
    return position()[2] // (fan // 2)


def split_two(value):
    high = value.astype(jnp.bfloat16)
    low = (value - high.astype(jnp.float32)).astype(jnp.bfloat16)
    return high, low


def linear_kernel(held, coef, lin, out):
    del out
    rows, width = held.shape
    weights = coef[...].reshape(1, width).astype(jnp.float32)
    step = min(512, rows)
    for i in range(0, rows, step):
        total = jnp.zeros((step, 128), jnp.float32)
        for j in range(0, width, 128):
            total = total + held[i : i + step, j : j + 128].astype(jnp.float32) * weights[:, j : j + 128]
        lin[:, i : i + step] = jnp.sum(total.T, axis=0, keepdims=True)


def spread(total, outs):
    size = outs[0].shape[0]
    for k, out in enumerate(outs):
        out[...] = total[k * size : (k + 1) * size]


def picks_kernel(per_dev, group, terms, effect, *refs):
    exposure, claims, ids, period, held, *far, picks = refs[terms:]
    cal, high, _, _ = position()
    base = cal * per_dev
    shift = jnp.zeros(claims.shape, jnp.float32)
    effects = effect[...].reshape(1, effect.shape[0])
    place = lax.broadcasted_iota(jnp.int32, effects.shape, 1)
    for k in range(per_dev):
        value = jnp.sum(jnp.where(place == base + k, effects, 0.0), axis=1, keepdims=True)
        shift = jnp.where(period[...] == base + k, value, shift)
    sums = [ref[...] for ref in refs[:terms]]
    while len(sums) > 1:
        sums = [a + b for a, b in zip(sums[::2], sums[1::2])]
    linear = sums[0]
    resid = claims[...] - jnp.exp(linear + exposure[...] + shift)
    resid = resid.astype(jnp.bfloat16).astype(jnp.float32)
    clusters, rows = picks.shape
    for k in range(clusters // group):
        first = (high ^ k) * group
        cluster = lax.broadcasted_iota(jnp.int32, (group, rows), 0) + first
        picks[k * group : (k + 1) * group, :] = jnp.where(cluster == ids[...], resid, 0.0).astype(jnp.bfloat16)
    half, deep = far[0].shape[1], clusters // 2
    columns = pl.ds(pl.multiple_of((1 - top_half()) * half, half), half)
    spread(jnp.dot(picks[deep:, :], held[:, columns], preferred_element_type=jnp.float32), far)


def rest_kernel(picks, held, *outs):
    half, group = outs[0].shape[1], outs[0].shape[0]
    deep = picks.shape[0] // 2
    columns = pl.ds(pl.multiple_of((1 - top_half()) * half, half), half)
    spread(jnp.dot(picks[:deep, :], held[:, columns], preferred_element_type=jnp.float32), outs[: deep // group])
    columns = pl.ds(pl.multiple_of(top_half() * half, half), half)
    spread(jnp.dot(picks[...], held[:, columns], preferred_element_type=jnp.float32), outs[deep // group :])


def meat_columns(scale, left, parts, store):
    high, low = split_two(jnp.concatenate([p[...] for p in parts], axis=0))
    deep = jnp.concatenate([high, high], axis=0)
    left_high = left[: left.shape[0] // 2]
    dims = (((0,), (0,)), ((), ()))
    half = high.shape[1]
    block = min(256, half)
    for n in range(half // block):
        part = slice(n * block, (n + 1) * block)
        total = lax.dot_general(
            left, deep[:, part], dims, preferred_element_type=jnp.float32
        ) + lax.dot_general(left_high, low[:, part], dims, preferred_element_type=jnp.float32)
        store(n, total * scale)


def own_kernel(scale, have, *refs):
    refs, (out, left) = refs[:-2], refs[-2:]
    got, own = refs[:-2], refs[-2:]
    _, high, _, gr = position()
    rows = jnp.where((gr ^ high) % 2 == 0, have[...], jnp.concatenate([ref[...] for ref in got], axis=0))
    both = jnp.concatenate(split_two(rows), axis=0)
    left[...] = both

    def store(n, value):
        out[n] = value

    meat_columns(scale, both, own, store)


def other_kernel(scale, first, left, *refs):
    other, (out, held, sems) = refs[:-3], refs[-3:]
    parts, _, block = held.shape
    copies = []

    def send(source, n, spot):
        columns = pl.ds(pl.multiple_of((spot * parts + n) * block, block), block)
        copies.append(pltpu.make_async_copy(source.at[n], out.at[:, columns], sems.at[len(copies)]))
        copies[-1].start()

    def store(n, value):
        held[n] = value
        send(held, n, 1 - top_half())

    for n in range(parts):
        send(first, n, top_half())
    meat_columns(scale, left[...], other, store)
    for copy in copies:
        copy.wait()


def exchange(value, cal_bits, gr_bits, n_cal, n_gr):
    pairs = [
        (c * n_gr + g, (c ^ cal_bits) * n_gr + (g ^ gr_bits))
        for c in range(n_cal)
        for g in range(n_gr)
    ]
    return lax.ppermute(value, AXES, pairs)


def per_device(features, coef, log_exposure, claims, cluster_id, period, period_effect):
    rows, width = features.shape
    n_cal, n_gr = lax.axis_size("cal"), lax.axis_size("gr")
    clusters = CL_DEV * n_cal
    per_dev = period_effect.shape[0] // n_cal
    fan = n_cal // n_gr
    cal, gr = lax.axis_index("cal"), lax.axis_index("gr")
    high, low = cal // fan, cal % fan
    swap = functools.partial(exchange, n_cal=n_cal, n_gr=n_gr)

    def kernel(body, out_shape, args, scalars, name, flops=0, alias={}):
        outs = out_shape if isinstance(out_shape, tuple) else (out_shape,)
        call = pl.pallas_call(
            body,
            out_shape=out_shape,
            in_specs=[SMEM] * scalars + [VMEM] * (len(args) - scalars),
            out_specs=tuple(VMEM for _ in outs) if isinstance(out_shape, tuple) else VMEM,
            compiler_params=pltpu.CompilerParams(vmem_limit_bytes=LIMIT),
            cost_estimate=pl.CostEstimate(flops=flops, bytes_accessed=flops // 256, transcendentals=0),
            name=name,
            input_output_aliases=alias,
        )
        return call(*args)

    f32, bf16 = jnp.float32, jnp.bfloat16
    lin, features = kernel(
        linear_kernel,
        (jax.ShapeDtypeStruct((1, rows), f32), jax.ShapeDtypeStruct((rows, width), bf16)),
        (features, coef), 0, "linear", 2 * rows * width, {0: 1},
    )
    linears = [lin] + [swap(lin, 0, k) for k in [*range(n_gr // 2, n_gr), *range(1, n_gr // 2)]]

    half = width // 2
    deep = clusters // 2
    group = clusters // n_gr
    flat = [v.reshape(1, rows) for v in (log_exposure, claims, cluster_id, period)]
    work = 2 * rows * deep * half
    score = jax.ShapeDtypeStruct((group, half), f32)
    *far, picks = kernel(
        functools.partial(picks_kernel, per_dev, group, n_gr),
        (score,) * (n_gr // 2) + (jax.ShapeDtypeStruct((clusters, rows), bf16),),
        (period_effect, *linears, *flat, features),
        0, "send_far", work,
    )
    far = [swap(value, fan // 2, 0) for value in far]
    rest = kernel(rest_kernel, (score,) * (n_gr // 2 + n_gr), (picks, features), 0, "rest", 3 * work)
    there = [swap(value, fan // 2, 0) for value in rest[: n_gr // 2]] + far
    kept = rest[n_gr // 2 :]
    parts = []
    for k in range(n_gr):
        part = kept[k] + there[k]
        bits = fan // 4
        while bits:
            size = part.shape[1] // 2
            mine = (low // bits) % 2
            away = lax.dynamic_slice_in_dim(part, (1 - mine) * size, size, axis=1)
            part = lax.dynamic_slice_in_dim(part, mine * size, size, axis=1) + swap(away, bits, 0)
            bits //= 2
        parts.append(part)

    arrived = {k: swap(parts[k], k * fan, 0) for k in range(n_gr - 1, 0, -1)}
    owned = lax.optimization_barrier(arrived[n_gr // 2] + arrived[n_gr // 2 + 1])
    for k in [*range(n_gr // 2 + 2, n_gr), *range(1, n_gr // 2)]:
        owned = owned + arrived[k]
    owned = owned + parts[0]
    gathered = [owned] + [swap(owned, k * fan, 0) for k in range(n_gr - 1, 0, -1)]
    blocks = [gathered[0], jnp.concatenate(gathered[1:], axis=0)]
    sides, others = [], []
    for side in blocks:
        bits = 1
        while bits < fan // 2:
            mine = (low // bits) % 2
            away = swap(side, bits, 0)
            side = jnp.where(
                mine == 0, jnp.concatenate([side, away], axis=1), jnp.concatenate([away, side], axis=1)
            )
            bits *= 2
        sides.append(side)
        others.append(swap(side, fan // 2, 0))

    have = jnp.concatenate(gathered, axis=0)
    have, others[0] = lax.optimization_barrier((have, others[0]))
    turn = gr ^ high
    bits = n_gr // 2
    while bits > 1:
        pairs = []
        for c in range(n_cal):
            for g in range(n_gr):
                step = (g ^ (c // fan)) & (2 * bits - 1)
                flip = bits if step == 0 or step == 2 * bits - 1 else bits // 2
                pairs.append((c * n_gr + g, c * n_gr + (g ^ flip)))
        if bits > 2:
            pairs = [(c * n_gr + g, c * n_gr + (g ^ bits)) for c in range(n_cal) for g in range(n_gr)]
        got = lax.ppermute(have, AXES, pairs)
        have = jnp.where((turn & bits) != 0, got, have)
        bits //= 2
    got = [swap(have[k * deep : (k + 1) * deep], 0, 1) for k in range(2)]
    scale = 1.0 / (rows * n_cal)
    wide, block = have.shape[1], min(256, half)
    parts = half // block
    work = 6 * clusters * half * wide
    first, left = kernel(
        functools.partial(own_kernel, scale),
        (jax.ShapeDtypeStruct((parts, wide, block), f32), jax.ShapeDtypeStruct((2 * clusters, wide), bf16)),
        (have, *got, *sides), 0, "meat_own", work,
    )
    args = (first, left, *others)
    return pl.pallas_call(
        functools.partial(other_kernel, scale),
        out_shape=jax.ShapeDtypeStruct((wide, width), f32),
        in_specs=[VMEM] * len(args),
        out_specs=ANY,
        scratch_shapes=[pltpu.VMEM((parts, wide, block), f32), pltpu.SemaphoreType.DMA((2 * parts,))],
        compiler_params=pltpu.CompilerParams(vmem_limit_bytes=LIMIT),
        cost_estimate=pl.CostEstimate(flops=work, bytes_accessed=4 * wide * width, transcendentals=0),
        name="meat_other",
    )(*args)


def solution(mesh):
    placed = (P("cal", "gr"), P("gr"), P("cal"), P("cal"), P("cal"), P("cal"), P())
    return jax.shard_map(
        per_device, mesh=mesh, in_specs=placed, out_specs=P("cal", "gr"), check_vma=False
    )
```

```python
import functools

import jax
import jax.numpy as jnp
from jax import lax
from jax.experimental import pallas as pl
from jax.experimental.pallas import tpu as pltpu
from jax.sharding import PartitionSpec as P

CL_DEV = 16
AXES = ("cal", "gr")
VMEM = pl.BlockSpec(memory_space=pltpu.VMEM)
SMEM = pl.BlockSpec(memory_space=pltpu.SMEM)
ANY = pl.BlockSpec(memory_space=pl.ANY)
LIMIT = 24 * 1024 * 1024


def position():
    fan = lax.axis_size("cal") // lax.axis_size("gr")
    cal, gr = lax.axis_index("cal"), lax.axis_index("gr")
    return cal, cal // fan, cal % fan, gr


def top_half():
    fan = lax.axis_size("cal") // lax.axis_size("gr")
    return position()[2] // (fan // 2)


def split_two(value):
    high = value.astype(jnp.bfloat16)
    low = (value - high.astype(jnp.float32)).astype(jnp.bfloat16)
    return high, low


def linear_kernel(held, coef, lin, out):
    del out
    rows, width = held.shape
    weights = coef[...].reshape(1, width).astype(jnp.float32)
    step = min(512, rows)
    for i in range(0, rows, step):
        total = jnp.zeros((step, 128), jnp.float32)
        for j in range(0, width, 128):
            total = total + held[i : i + step, j : j + 128].astype(jnp.float32) * weights[:, j : j + 128]
        lin[:, i : i + step] = jnp.sum(total.T, axis=0, keepdims=True)


def spread(total, outs):
    size = outs[0].shape[0]
    for k, out in enumerate(outs):
        out[...] = total[k * size : (k + 1) * size]


def picks_kernel(per_dev, group, terms, effect, *refs):
    exposure, claims, ids, period, held, *far, picks = refs[terms:]
    cal, high, _, _ = position()
    base = cal * per_dev
    shift = jnp.zeros(claims.shape, jnp.float32)
    effects = effect[...].reshape(1, effect.shape[0])
    place = lax.broadcasted_iota(jnp.int32, effects.shape, 1)
    for k in range(per_dev):
        value = jnp.sum(jnp.where(place == base + k, effects, 0.0), axis=1, keepdims=True)
        shift = jnp.where(period[...] == base + k, value, shift)
    sums = [ref[...] for ref in refs[:terms]]
    while len(sums) > 1:
        sums = [a + b for a, b in zip(sums[::2], sums[1::2])]
    linear = sums[0]
    resid = claims[...] - jnp.exp(linear + exposure[...] + shift)
    resid = resid.astype(jnp.bfloat16).astype(jnp.float32)
    clusters, rows = picks.shape
    for k in range(clusters // group):
        first = (high ^ k) * group
        cluster = lax.broadcasted_iota(jnp.int32, (group, rows), 0) + first
        picks[k * group : (k + 1) * group, :] = jnp.where(cluster == ids[...], resid, 0.0).astype(jnp.bfloat16)
    half, deep = far[0].shape[1], clusters // 2
    columns = pl.ds(pl.multiple_of((1 - top_half()) * half, half), half)
    spread(jnp.dot(picks[deep:, :], held[:, columns], preferred_element_type=jnp.float32), far)


def rest_kernel(picks, held, *outs):
    half, group = outs[0].shape[1], outs[0].shape[0]
    deep = picks.shape[0] // 2
    columns = pl.ds(pl.multiple_of((1 - top_half()) * half, half), half)
    spread(jnp.dot(picks[:deep, :], held[:, columns], preferred_element_type=jnp.float32), outs[: deep // group])
    columns = pl.ds(pl.multiple_of(top_half() * half, half), half)
    spread(jnp.dot(picks[...], held[:, columns], preferred_element_type=jnp.float32), outs[deep // group :])


def meat_columns(scale, left, parts, store):
    high, low = split_two(jnp.concatenate([p[...] for p in parts], axis=0))
    deep = jnp.concatenate([high, high], axis=0)
    left_high = left[: left.shape[0] // 2]
    dims = (((0,), (0,)), ((), ()))
    half = high.shape[1]
    block = min(256, half)
    for n in range(half // block):
        part = slice(n * block, (n + 1) * block)
        total = lax.dot_general(
            left, deep[:, part], dims, preferred_element_type=jnp.float32
        ) + lax.dot_general(left_high, low[:, part], dims, preferred_element_type=jnp.float32)
        store(n, total * scale)


def own_kernel(scale, have, *refs):
    refs, (out, left) = refs[:-2], refs[-2:]
    got, own = refs[:-2], refs[-2:]
    _, high, _, gr = position()
    rows = jnp.where((gr ^ high) % 2 == 0, have[...], jnp.concatenate([ref[...] for ref in got], axis=0))
    both = jnp.concatenate(split_two(rows), axis=0)
    left[...] = both

    def store(n, value):
        out[n] = value

    meat_columns(scale, both, own, store)


def other_kernel(scale, first, left, *refs):
    other, (out, held, sems) = refs[:-3], refs[-3:]
    parts, _, block = held.shape
    copies = []

    def send(source, n, spot):
        columns = pl.ds(pl.multiple_of((spot * parts + n) * block, block), block)
        copies.append(pltpu.make_async_copy(source.at[n], out.at[:, columns], sems.at[len(copies)]))
        copies[-1].start()

    def store(n, value):
        held[n] = value
        send(held, n, 1 - top_half())

    for n in range(parts):
        send(first, n, top_half())
    meat_columns(scale, left[...], other, store)
    for copy in copies:
        copy.wait()


def exchange(value, cal_bits, gr_bits, n_cal, n_gr):
    pairs = [
        (c * n_gr + g, (c ^ cal_bits) * n_gr + (g ^ gr_bits))
        for c in range(n_cal)
        for g in range(n_gr)
    ]
    return lax.ppermute(value, AXES, pairs)


def per_device(features, coef, log_exposure, claims, cluster_id, period, period_effect):
    rows, width = features.shape
    n_cal, n_gr = lax.axis_size("cal"), lax.axis_size("gr")
    clusters = CL_DEV * n_cal
    per_dev = period_effect.shape[0] // n_cal
    fan = n_cal // n_gr
    cal, gr = lax.axis_index("cal"), lax.axis_index("gr")
    high, low = cal // fan, cal % fan
    swap = functools.partial(exchange, n_cal=n_cal, n_gr=n_gr)

    def kernel(body, out_shape, args, scalars, name, flops=0, alias={}):
        outs = out_shape if isinstance(out_shape, tuple) else (out_shape,)
        call = pl.pallas_call(
            body,
            out_shape=out_shape,
            in_specs=[SMEM] * scalars + [VMEM] * (len(args) - scalars),
            out_specs=tuple(VMEM for _ in outs) if isinstance(out_shape, tuple) else VMEM,
            compiler_params=pltpu.CompilerParams(vmem_limit_bytes=LIMIT),
            cost_estimate=pl.CostEstimate(flops=flops, bytes_accessed=flops // 256, transcendentals=0),
            name=name,
            input_output_aliases=alias,
        )
        return call(*args)

    f32, bf16 = jnp.float32, jnp.bfloat16
    lin, features = kernel(
        linear_kernel,
        (jax.ShapeDtypeStruct((1, rows), f32), jax.ShapeDtypeStruct((rows, width), bf16)),
        (features, coef), 0, "linear", 2 * rows * width, {0: 1},
    )
    linears = [lin] + [swap(lin, 0, k) for k in [*range(n_gr // 2, n_gr), *range(1, n_gr // 2)]]

    half = width // 2
    deep = clusters // 2
    group = clusters // n_gr
    flat = [v.reshape(1, rows) for v in (log_exposure, claims, cluster_id, period)]
    work = 2 * rows * deep * half
    score = jax.ShapeDtypeStruct((group, half), f32)
    *far, picks = kernel(
        functools.partial(picks_kernel, per_dev, group, n_gr),
        (score,) * (n_gr // 2) + (jax.ShapeDtypeStruct((clusters, rows), bf16),),
        (period_effect, *linears, *flat, features),
        0, "send_far", work,
    )
    far = [swap(value, fan // 2, 0) for value in far]
    rest = kernel(rest_kernel, (score,) * (n_gr // 2 + n_gr), (picks, features), 0, "rest", 3 * work)
    there = [swap(value, fan // 2, 0) for value in rest[: n_gr // 2]] + far
    kept = rest[n_gr // 2 :]
    parts = []
    for k in range(n_gr):
        part = kept[k] + there[k]
        bits = fan // 4
        while bits:
            size = part.shape[1] // 2
            mine = (low // bits) % 2
            away = lax.dynamic_slice_in_dim(part, (1 - mine) * size, size, axis=1)
            part = lax.dynamic_slice_in_dim(part, mine * size, size, axis=1) + swap(away, bits, 0)
            bits //= 2
        parts.append(part)

    arrived = {k: swap(parts[k], k * fan, 0) for k in range(n_gr - 1, 0, -1)}
    owned = lax.optimization_barrier(arrived[n_gr // 2] + arrived[n_gr // 2 + 1])
    for k in [*range(n_gr // 2 + 2, n_gr), *range(1, n_gr // 2)]:
        owned = owned + arrived[k]
    owned = owned + parts[0]
    gathered = [owned] + [swap(owned, k * fan, 0) for k in [3, 2, 1]]
    blocks = [jnp.concatenate(gathered[0:2], axis=0), jnp.concatenate(gathered[2:4], axis=0)]
    sides, others = [], []
    for side in blocks:
        bits = 1
        while bits < fan // 2:
            mine = (low // bits) % 2
            away = swap(side, bits, 0)
            side = jnp.where(
                mine == 0, jnp.concatenate([side, away], axis=1), jnp.concatenate([away, side], axis=1)
            )
            bits *= 2
        sides.append(side)
        others.append(swap(side, fan // 2, 0))

    have = jnp.concatenate(gathered, axis=0)
    turn = gr ^ high
    bits = n_gr // 2
    while bits > 1:
        pairs = []
        for c in range(n_cal):
            for g in range(n_gr):
                step = (g ^ (c // fan)) & (2 * bits - 1)
                flip = bits if step == 0 or step == 2 * bits - 1 else bits // 2
                pairs.append((c * n_gr + g, c * n_gr + (g ^ flip)))
        if bits > 2:
            pairs = [(c * n_gr + g, c * n_gr + (g ^ bits)) for c in range(n_cal) for g in range(n_gr)]
        got = jnp.concatenate([lax.ppermute(have[i : i + clusters // 4], AXES, pairs) for i in range(0, clusters, clusters // 4)], axis=0)
        got, *others[:1] = lax.optimization_barrier((got, *others[:1]))
        have = jnp.where((turn & bits) != 0, got, have)
        bits //= 2
    got = [swap(have[i : i + clusters // 4], 0, 1) for i in range(0, clusters, clusters // 4)]
    scale = 1.0 / (rows * n_cal)
    wide, block = have.shape[1], min(256, half)
    parts = half // block
    work = 6 * clusters * half * wide
    first, left = kernel(
        functools.partial(own_kernel, scale),
        (jax.ShapeDtypeStruct((parts, wide, block), f32), jax.ShapeDtypeStruct((2 * clusters, wide), bf16)),
        (have, *got, *sides), 0, "meat_own", work,
    )
    args = (first, left, *others)
    return pl.pallas_call(
        functools.partial(other_kernel, scale),
        out_shape=jax.ShapeDtypeStruct((wide, width), f32),
        in_specs=[VMEM] * len(args),
        out_specs=ANY,
        scratch_shapes=[pltpu.VMEM((parts, wide, block), f32), pltpu.SemaphoreType.DMA((2 * parts,))],
        compiler_params=pltpu.CompilerParams(vmem_limit_bytes=LIMIT),
        cost_estimate=pl.CostEstimate(flops=work, bytes_accessed=4 * wide * width, transcendentals=0),
        name="meat_other",
    )(*args)


def solution(mesh):
    placed = (P("cal", "gr"), P("gr"), P("cal"), P("cal"), P("cal"), P("cal"), P())
    return jax.shard_map(
        per_device, mesh=mesh, in_specs=placed, out_specs=P("cal", "gr"), check_vma=False
    )
```

```python
import functools

import jax
import jax.numpy as jnp
from jax import lax
from jax.experimental import pallas as pl
from jax.experimental.pallas import tpu as pltpu
from jax.sharding import PartitionSpec as P

CL_DEV = 16
AXES = ("cal", "gr")
VMEM = pl.BlockSpec(memory_space=pltpu.VMEM)
SMEM = pl.BlockSpec(memory_space=pltpu.SMEM)
ANY = pl.BlockSpec(memory_space=pl.ANY)
LIMIT = 24 * 1024 * 1024


def position():
    fan = lax.axis_size("cal") // lax.axis_size("gr")
    cal, gr = lax.axis_index("cal"), lax.axis_index("gr")
    return cal, cal // fan, cal % fan, gr


def top_half():
    fan = lax.axis_size("cal") // lax.axis_size("gr")
    return position()[2] // (fan // 2)


def split_two(value):
    high = value.astype(jnp.bfloat16)
    low = (value - high.astype(jnp.float32)).astype(jnp.bfloat16)
    return high, low


def linear_kernel(feats, coef, lin, held, weights, sems):
    rows, width = held.shape
    step = min(512, rows)
    fetch = pltpu.make_async_copy(coef, weights, sems.at[rows // step])
    fetch.start()
    copies = []
    for i in range(0, rows, step):
        part = pl.ds(i, step)
        copies.append(pltpu.make_async_copy(feats.at[part], held.at[part], sems.at[i // step]))
        copies[-1].start()
    fetch.wait()
    scale = weights[...].reshape(1, width).astype(jnp.float32)
    for i in range(0, rows, step):
        copies[i // step].wait()
        total = jnp.zeros((step, 128), jnp.float32)
        for j in range(0, width, 128):
            total = total + held[i : i + step, j : j + 128].astype(jnp.float32) * scale[:, j : j + 128]
        lin[:, i : i + step] = jnp.sum(total.T, axis=0, keepdims=True)


def spread(total, outs):
    size = outs[0].shape[0]
    for k, out in enumerate(outs):
        out[...] = total[k * size : (k + 1) * size]


def picks_kernel(per_dev, group, terms, effect, *refs):
    exposure, claims, ids, period, held, *far, picks = refs[terms:]
    cal, high, _, _ = position()
    base = cal * per_dev
    shift = jnp.zeros(claims.shape, jnp.float32)
    effects = effect[...].reshape(1, effect.shape[0])
    place = lax.broadcasted_iota(jnp.int32, effects.shape, 1)
    for k in range(per_dev):
        value = jnp.sum(jnp.where(place == base + k, effects, 0.0), axis=1, keepdims=True)
        shift = jnp.where(period[...] == base + k, value, shift)
    sums = [ref[...] for ref in refs[:terms]]
    while len(sums) > 1:
        sums = [a + b for a, b in zip(sums[::2], sums[1::2])]
    linear = sums[0]
    resid = claims[...] - jnp.exp(linear + exposure[...] + shift)
    resid = resid.astype(jnp.bfloat16).astype(jnp.float32)
    clusters, rows = picks.shape
    for k in range(clusters // group):
        first = (high ^ k) * group
        cluster = lax.broadcasted_iota(jnp.int32, (group, rows), 0) + first
        picks[k * group : (k + 1) * group, :] = jnp.where(cluster == ids[...], resid, 0.0).astype(jnp.bfloat16)
    half, deep = far[0].shape[1], clusters // 2
    columns = pl.ds(pl.multiple_of((1 - top_half()) * half, half), half)
    spread(jnp.dot(picks[deep:, :], held[:, columns], preferred_element_type=jnp.float32), far)


def rest_kernel(picks, held, *outs):
    half, group = outs[0].shape[1], outs[0].shape[0]
    deep = picks.shape[0] // 2
    columns = pl.ds(pl.multiple_of((1 - top_half()) * half, half), half)
    spread(jnp.dot(picks[:deep, :], held[:, columns], preferred_element_type=jnp.float32), outs[: deep // group])
    columns = pl.ds(pl.multiple_of(top_half() * half, half), half)
    spread(jnp.dot(picks[...], held[:, columns], preferred_element_type=jnp.float32), outs[deep // group :])


def meat_columns(scale, left, parts, store):
    high, low = split_two(jnp.concatenate([p[...] for p in parts], axis=0))
    deep = jnp.concatenate([high, high], axis=0)
    left_high = left[: left.shape[0] // 2]
    dims = (((0,), (0,)), ((), ()))
    half = high.shape[1]
    block = min(256, half)
    for n in range(half // block):
        part = slice(n * block, (n + 1) * block)
        total = lax.dot_general(
            left, deep[:, part], dims, preferred_element_type=jnp.float32
        ) + lax.dot_general(left_high, low[:, part], dims, preferred_element_type=jnp.float32)
        store(n, total * scale)


def own_kernel(scale, have, *refs):
    refs, (out, left) = refs[:-2], refs[-2:]
    got, own = refs[:-2], refs[-2:]
    _, high, _, gr = position()
    rows = jnp.where((gr ^ high) % 2 == 0, have[...], jnp.concatenate([ref[...] for ref in got], axis=0))
    both = jnp.concatenate(split_two(rows), axis=0)
    left[...] = both

    def store(n, value):
        out[n] = value

    meat_columns(scale, both, own, store)


def other_kernel(scale, first, left, *refs):
    other, (out, held, sems) = refs[:-3], refs[-3:]
    parts, _, block = held.shape
    copies = []

    def send(source, n, spot):
        columns = pl.ds(pl.multiple_of((spot * parts + n) * block, block), block)
        copies.append(pltpu.make_async_copy(source.at[n], out.at[:, columns], sems.at[len(copies)]))
        copies[-1].start()

    def store(n, value):
        held[n] = value
        send(held, n, 1 - top_half())

    for n in range(parts):
        send(first, n, top_half())
    meat_columns(scale, left[...], other, store)
    for copy in copies:
        copy.wait()


def exchange(value, cal_bits, gr_bits, n_cal, n_gr):
    pairs = [
        (c * n_gr + g, (c ^ cal_bits) * n_gr + (g ^ gr_bits))
        for c in range(n_cal)
        for g in range(n_gr)
    ]
    return lax.ppermute(value, AXES, pairs)


def per_device(features, coef, log_exposure, claims, cluster_id, period, period_effect):
    rows, width = features.shape
    n_cal, n_gr = lax.axis_size("cal"), lax.axis_size("gr")
    clusters = CL_DEV * n_cal
    per_dev = period_effect.shape[0] // n_cal
    fan = n_cal // n_gr
    cal, gr = lax.axis_index("cal"), lax.axis_index("gr")
    high, low = cal // fan, cal % fan
    swap = functools.partial(exchange, n_cal=n_cal, n_gr=n_gr)

    def kernel(body, out_shape, args, scalars, name, flops=0, alias={}):
        outs = out_shape if isinstance(out_shape, tuple) else (out_shape,)
        call = pl.pallas_call(
            body,
            out_shape=out_shape,
            in_specs=[SMEM] * scalars + [VMEM] * (len(args) - scalars),
            out_specs=tuple(VMEM for _ in outs) if isinstance(out_shape, tuple) else VMEM,
            compiler_params=pltpu.CompilerParams(vmem_limit_bytes=LIMIT),
            cost_estimate=pl.CostEstimate(flops=flops, bytes_accessed=flops // 256, transcendentals=0),
            name=name,
            input_output_aliases=alias,
        )
        return call(*args)

    f32, bf16 = jnp.float32, jnp.bfloat16
    pieces = rows // min(512, rows)
    lin, features = pl.pallas_call(
        linear_kernel,
        out_shape=(jax.ShapeDtypeStruct((1, rows), f32), jax.ShapeDtypeStruct((rows, width), bf16)),
        in_specs=[ANY, ANY],
        out_specs=(VMEM, VMEM),
        scratch_shapes=[pltpu.VMEM((width,), bf16), pltpu.SemaphoreType.DMA((pieces + 1,))],
        compiler_params=pltpu.CompilerParams(vmem_limit_bytes=LIMIT),
        cost_estimate=pl.CostEstimate(flops=2 * rows * width, bytes_accessed=2 * rows * width, transcendentals=0),
        name="linear",
    )(*(pltpu.with_memory_space_constraint(value, pltpu.HBM) for value in (features, coef)))
    linears = [lin] + [swap(lin, 0, k) for k in [*range(n_gr // 2, n_gr), *range(1, n_gr // 2)]]

    half = width // 2
    deep = clusters // 2
    group = clusters // n_gr
    flat = [v.reshape(1, rows) for v in (log_exposure, claims, cluster_id, period)]
    work = 2 * rows * deep * half
    score = jax.ShapeDtypeStruct((group, half), f32)
    *far, picks = kernel(
        functools.partial(picks_kernel, per_dev, group, n_gr),
        (score,) * (n_gr // 2) + (jax.ShapeDtypeStruct((clusters, rows), bf16),),
        (period_effect, *linears, *flat, features),
        0, "send_far", work,
    )
    far = [swap(value, fan // 2, 0) for value in far]
    rest = kernel(rest_kernel, (score,) * (n_gr // 2 + n_gr), (picks, features), 0, "rest", 3 * work)
    there = [swap(value, fan // 2, 0) for value in rest[: n_gr // 2]] + far
    kept = rest[n_gr // 2 :]
    parts = []
    for k in range(n_gr):
        part = kept[k] + there[k]
        bits = fan // 4
        while bits:
            size = part.shape[1] // 2
            mine = (low // bits) % 2
            away = lax.dynamic_slice_in_dim(part, (1 - mine) * size, size, axis=1)
            part = lax.dynamic_slice_in_dim(part, mine * size, size, axis=1) + swap(away, bits, 0)
            bits //= 2
        parts.append(part)

    arrived = {k: swap(parts[k], k * fan, 0) for k in range(n_gr - 1, 0, -1)}
    owned = lax.optimization_barrier(arrived[n_gr // 2] + arrived[n_gr // 2 + 1])
    for k in [*range(n_gr // 2 + 2, n_gr), *range(1, n_gr // 2)]:
        owned = owned + arrived[k]
    owned = owned + parts[0]
    gathered = [owned] + [swap(owned, k * fan, 0) for k in [3, 1, 2]]
    blocks = [jnp.concatenate(gathered[0:2], axis=0), jnp.concatenate(gathered[2:4], axis=0)]
    sides, others = [], []
    for side in blocks:
        bits = 1
        while bits < fan // 2:
            mine = (low // bits) % 2
            away = swap(side, bits, 0)
            side = jnp.where(
                mine == 0, jnp.concatenate([side, away], axis=1), jnp.concatenate([away, side], axis=1)
            )
            bits *= 2
        sides.append(side)
        others.append(swap(side, fan // 2, 0))

    have = jnp.concatenate(gathered, axis=0)
    turn = gr ^ high
    bits = n_gr // 2
    while bits > 1:
        pairs = []
        for c in range(n_cal):
            for g in range(n_gr):
                step = (g ^ (c // fan)) & (2 * bits - 1)
                flip = bits if step == 0 or step == 2 * bits - 1 else bits // 2
                pairs.append((c * n_gr + g, c * n_gr + (g ^ flip)))
        if bits > 2:
            pairs = [(c * n_gr + g, c * n_gr + (g ^ bits)) for c in range(n_cal) for g in range(n_gr)]
        got = jnp.concatenate([lax.ppermute(have[i : i + clusters // 4], AXES, pairs) for i in range(0, clusters, clusters // 4)], axis=0)
        got, *others[:1] = lax.optimization_barrier((got, *others[:1]))
        have = jnp.where((turn & bits) != 0, got, have)
        bits //= 2
    got = [swap(have[i : i + clusters // 4], 0, 1) for i in range(0, clusters, clusters // 4)]
    scale = 1.0 / (rows * n_cal)
    wide, block = have.shape[1], min(256, half)
    parts = half // block
    work = 6 * clusters * half * wide
    first, left = kernel(
        functools.partial(own_kernel, scale),
        (jax.ShapeDtypeStruct((parts, wide, block), f32), jax.ShapeDtypeStruct((2 * clusters, wide), bf16)),
        (have, *got, *sides), 0, "meat_own", work,
    )
    args = (first, left, *others)
    return pl.pallas_call(
        functools.partial(other_kernel, scale),
        out_shape=jax.ShapeDtypeStruct((wide, width), f32),
        in_specs=[VMEM] * len(args),
        out_specs=ANY,
        scratch_shapes=[pltpu.VMEM((parts, wide, block), f32), pltpu.SemaphoreType.DMA((2 * parts,))],
        compiler_params=pltpu.CompilerParams(vmem_limit_bytes=LIMIT),
        cost_estimate=pl.CostEstimate(flops=work, bytes_accessed=4 * wide * width, transcendentals=0),
        name="meat_other",
    )(*args)


def solution(mesh):
    placed = (P("cal", "gr"), P("gr"), P("cal"), P("cal"), P("cal"), P("cal"), P())
    return jax.shard_map(
        per_device, mesh=mesh, in_specs=placed, out_specs=P("cal", "gr"), check_vma=False
    )
```

```python
import functools

import jax
import jax.numpy as jnp
from jax import lax
from jax.experimental import pallas as pl
from jax.experimental.pallas import tpu as pltpu
from jax.sharding import PartitionSpec as P

CL_DEV = 16
AXES = ("cal", "gr")
VMEM = pl.BlockSpec(memory_space=pltpu.VMEM)
SMEM = pl.BlockSpec(memory_space=pltpu.SMEM)
ANY = pl.BlockSpec(memory_space=pl.ANY)
LIMIT = 24 * 1024 * 1024


def position():
    fan = lax.axis_size("cal") // lax.axis_size("gr")
    cal, gr = lax.axis_index("cal"), lax.axis_index("gr")
    return cal, cal // fan, cal % fan, gr


def top_half():
    fan = lax.axis_size("cal") // lax.axis_size("gr")
    return position()[2] // (fan // 2)


def split_two(value):
    high = value.astype(jnp.bfloat16)
    low = (value - high.astype(jnp.float32)).astype(jnp.bfloat16)
    return high, low


def linear_kernel(feats, coef, lin, held, weights, sems):
    rows, width = held.shape
    step = min(512, rows)
    fetch = pltpu.make_async_copy(coef, weights, sems.at[rows // step])
    fetch.start()
    copies = []
    for i in range(0, rows, step):
        part = pl.ds(i, step)
        copies.append(pltpu.make_async_copy(feats.at[part], held.at[part], sems.at[i // step]))
        copies[-1].start()
    fetch.wait()
    scale = weights[...].reshape(1, width).astype(jnp.float32)
    for i in range(0, rows, step):
        copies[i // step].wait()
        total = jnp.zeros((step, 128), jnp.float32)
        for j in range(0, width, 128):
            total = total + held[i : i + step, j : j + 128].astype(jnp.float32) * scale[:, j : j + 128]
        lin[:, i : i + step] = jnp.sum(total.T, axis=0, keepdims=True)


def spread(total, outs):
    size = outs[0].shape[0]
    for k, out in enumerate(outs):
        out[...] = total[k * size : (k + 1) * size]


def picks_kernel(per_dev, group, terms, effect, *refs):
    exposure, claims, ids, period, held, *far, picks = refs[terms:]
    cal, high, _, _ = position()
    base = cal * per_dev
    shift = jnp.zeros(claims.shape, jnp.float32)
    effects = effect[...].reshape(1, effect.shape[0])
    place = lax.broadcasted_iota(jnp.int32, effects.shape, 1)
    for k in range(per_dev):
        value = jnp.sum(jnp.where(place == base + k, effects, 0.0), axis=1, keepdims=True)
        shift = jnp.where(period[...] == base + k, value, shift)
    sums = [ref[...] for ref in refs[:terms]]
    while len(sums) > 1:
        sums = [a + b for a, b in zip(sums[::2], sums[1::2])]
    linear = sums[0]
    resid = claims[...] - jnp.exp(linear + exposure[...] + shift)
    resid = resid.astype(jnp.bfloat16).astype(jnp.float32)
    clusters, rows = picks.shape
    for k in range(clusters // group):
        first = (high ^ k) * group
        cluster = lax.broadcasted_iota(jnp.int32, (group, rows), 0) + first
        picks[k * group : (k + 1) * group, :] = jnp.where(cluster == ids[...], resid, 0.0).astype(jnp.bfloat16)
    half, deep = far[0].shape[1], clusters // 2
    columns = pl.ds(pl.multiple_of((1 - top_half()) * half, half), half)
    spread(jnp.dot(picks[deep:, :], held[:, columns], preferred_element_type=jnp.float32), far)


def rest_kernel(picks, held, *outs):
    half, group = outs[0].shape[1], outs[0].shape[0]
    deep = picks.shape[0] // 2
    columns = pl.ds(pl.multiple_of((1 - top_half()) * half, half), half)
    spread(jnp.dot(picks[:deep, :], held[:, columns], preferred_element_type=jnp.float32), outs[: deep // group])
    columns = pl.ds(pl.multiple_of(top_half() * half, half), half)
    spread(jnp.dot(picks[...], held[:, columns], preferred_element_type=jnp.float32), outs[deep // group :])


def meat_columns(scale, left, parts, store):
    high, low = split_two(jnp.concatenate([p[...] for p in parts], axis=0))
    deep = jnp.concatenate([high, high], axis=0)
    left_high = left[: left.shape[0] // 2]
    dims = (((0,), (0,)), ((), ()))
    half = high.shape[1]
    block = min(256, half)
    for n in range(half // block):
        part = slice(n * block, (n + 1) * block)
        total = lax.dot_general(
            left, deep[:, part], dims, preferred_element_type=jnp.float32
        ) + lax.dot_general(left_high, low[:, part], dims, preferred_element_type=jnp.float32)
        store(n, total * scale)


def own_kernel(scale, have, *refs):
    refs, (out, left) = refs[:-2], refs[-2:]
    got, own = refs[:-2], refs[-2:]
    _, high, _, gr = position()
    rows = jnp.where((gr ^ high) % 2 == 0, have[...], jnp.concatenate([ref[...] for ref in got], axis=0))
    both = jnp.concatenate(split_two(rows), axis=0)
    left[...] = both

    def store(n, value):
        out[n] = value

    meat_columns(scale, both, own, store)


def other_kernel(scale, first, left, *refs):
    other, (out, held, sems) = refs[:-3], refs[-3:]
    parts, _, block = held.shape
    copies = []

    def send(source, n, spot):
        columns = pl.ds(pl.multiple_of((spot * parts + n) * block, block), block)
        copies.append(pltpu.make_async_copy(source.at[n], out.at[:, columns], sems.at[len(copies)]))
        copies[-1].start()

    def store(n, value):
        held[n] = value
        send(held, n, 1 - top_half())

    for n in range(parts):
        send(first, n, top_half())
    meat_columns(scale, left[...], other, store)
    for copy in copies:
        copy.wait()


def exchange(value, cal_bits, gr_bits, n_cal, n_gr):
    pairs = [
        (c * n_gr + g, (c ^ cal_bits) * n_gr + (g ^ gr_bits))
        for c in range(n_cal)
        for g in range(n_gr)
    ]
    return lax.ppermute(value, AXES, pairs)


def per_device(features, coef, log_exposure, claims, cluster_id, period, period_effect):
    rows, width = features.shape
    n_cal, n_gr = lax.axis_size("cal"), lax.axis_size("gr")
    clusters = CL_DEV * n_cal
    per_dev = period_effect.shape[0] // n_cal
    fan = n_cal // n_gr
    cal, gr = lax.axis_index("cal"), lax.axis_index("gr")
    high, low = cal // fan, cal % fan
    swap = functools.partial(exchange, n_cal=n_cal, n_gr=n_gr)

    def kernel(body, out_shape, args, scalars, name, flops=0, alias={}):
        outs = out_shape if isinstance(out_shape, tuple) else (out_shape,)
        call = pl.pallas_call(
            body,
            out_shape=out_shape,
            in_specs=[SMEM] * scalars + [VMEM] * (len(args) - scalars),
            out_specs=tuple(VMEM for _ in outs) if isinstance(out_shape, tuple) else VMEM,
            compiler_params=pltpu.CompilerParams(vmem_limit_bytes=LIMIT),
            cost_estimate=pl.CostEstimate(flops=flops, bytes_accessed=flops // 256, transcendentals=0),
            name=name,
            input_output_aliases=alias,
        )
        return call(*args)

    f32, bf16 = jnp.float32, jnp.bfloat16
    pieces = rows // min(512, rows)
    lin, features = pl.pallas_call(
        linear_kernel,
        out_shape=(jax.ShapeDtypeStruct((1, rows), f32), jax.ShapeDtypeStruct((rows, width), bf16)),
        in_specs=[ANY, ANY],
        out_specs=(VMEM, VMEM),
        scratch_shapes=[pltpu.VMEM((width,), bf16), pltpu.SemaphoreType.DMA((pieces + 1,))],
        compiler_params=pltpu.CompilerParams(vmem_limit_bytes=LIMIT),
        cost_estimate=pl.CostEstimate(flops=2 * rows * width, bytes_accessed=2 * rows * width, transcendentals=0),
        name="linear",
    )(*(pltpu.with_memory_space_constraint(value, pltpu.HBM) for value in (features, coef)))
    linears = [lin] + [swap(lin, 0, k) for k in [*range(n_gr // 2, n_gr), *range(1, n_gr // 2)]]

    half = width // 2
    deep = clusters // 2
    group = clusters // n_gr
    flat = [v.reshape(1, rows) for v in (log_exposure, claims, cluster_id, period)]
    work = 2 * rows * deep * half
    score = jax.ShapeDtypeStruct((group, half), f32)
    *far, picks = kernel(
        functools.partial(picks_kernel, per_dev, group, n_gr),
        (score,) * (n_gr // 2) + (jax.ShapeDtypeStruct((clusters, rows), bf16),),
        (period_effect, *linears, *flat, features),
        0, "send_far", work,
    )
    far = [swap(value, fan // 2, 0) for value in far]
    rest = kernel(rest_kernel, (score,) * (n_gr // 2 + n_gr), (picks, features), 0, "rest", 3 * work)
    there = [swap(value, fan // 2, 0) for value in rest[: n_gr // 2]] + far
    kept = rest[n_gr // 2 :]
    parts = []
    for k in range(n_gr):
        part = kept[k] + there[k]
        bits = fan // 4
        while bits:
            size = part.shape[1] // 2
            mine = (low // bits) % 2
            away = lax.dynamic_slice_in_dim(part, (1 - mine) * size, size, axis=1)
            part = lax.dynamic_slice_in_dim(part, mine * size, size, axis=1) + swap(away, bits, 0)
            bits //= 2
        parts.append(part)

    arrived = {k: swap(parts[k], k * fan, 0) for k in range(n_gr - 1, 0, -1)}
    owned = lax.optimization_barrier(arrived[n_gr // 2] + arrived[n_gr // 2 + 1])
    for k in [*range(n_gr // 2 + 2, n_gr), *range(1, n_gr // 2)]:
        owned = owned + arrived[k]
    owned = owned + parts[0]
    def along(value, k):
        table = [[2, 0, 3, 1], [1, 3, 0, 2], [3, 2, 1, 0]][k]
        pairs = []
        for c in range(n_cal):
            there = (table[c // fan] if n_gr == 4 else (c // fan) ^ (k + 1)) * fan + c % fan
            pairs += [(c * n_gr + g, there * n_gr + g) for g in range(n_gr)]
        return lax.ppermute(value, AXES, pairs)

    gathered = [owned] + [along(owned, k) for k in range(n_gr - 1)]
    blocks = [jnp.concatenate(gathered[0:2], axis=0), jnp.concatenate(gathered[2:4], axis=0)]
    sides, others = [], []
    for side in blocks:
        bits = 1
        while bits < fan // 2:
            mine = (low // bits) % 2
            away = swap(side, bits, 0)
            side = jnp.where(
                mine == 0, jnp.concatenate([side, away], axis=1), jnp.concatenate([away, side], axis=1)
            )
            bits *= 2
        sides.append(side)
        others.append(swap(side, fan // 2, 0))

    have = jnp.concatenate(gathered, axis=0)
    turn = gr ^ high
    bits = n_gr // 2
    while bits > 1:
        pairs = []
        for c in range(n_cal):
            for g in range(n_gr):
                step = (g ^ (c // fan)) & (2 * bits - 1)
                flip = bits if step == 0 or step == 2 * bits - 1 else bits // 2
                pairs.append((c * n_gr + g, c * n_gr + (g ^ flip)))
        if bits > 2:
            pairs = [(c * n_gr + g, c * n_gr + (g ^ bits)) for c in range(n_cal) for g in range(n_gr)]
        got = jnp.concatenate([lax.ppermute(have[i : i + clusters // 4], AXES, pairs) for i in range(0, clusters, clusters // 4)], axis=0)
        got, *others[:1] = lax.optimization_barrier((got, *others[:1]))
        have = jnp.where((turn & bits) != 0, got, have)
        bits //= 2
    got = [swap(have[i : i + clusters // 4], 0, 1) for i in range(0, clusters, clusters // 4)]
    scale = 1.0 / (rows * n_cal)
    wide, block = have.shape[1], min(256, half)
    parts = half // block
    work = 6 * clusters * half * wide
    first, left = kernel(
        functools.partial(own_kernel, scale),
        (jax.ShapeDtypeStruct((parts, wide, block), f32), jax.ShapeDtypeStruct((2 * clusters, wide), bf16)),
        (have, *got, *sides), 0, "meat_own",
    )
    args = (first, left, *others)
    return pl.pallas_call(
        functools.partial(other_kernel, scale),
        out_shape=jax.ShapeDtypeStruct((wide, width), f32),
        in_specs=[VMEM] * len(args),
        out_specs=ANY,
        scratch_shapes=[pltpu.VMEM((parts, wide, block), f32), pltpu.SemaphoreType.DMA((2 * parts,))],
        compiler_params=pltpu.CompilerParams(vmem_limit_bytes=LIMIT),
        cost_estimate=pl.CostEstimate(flops=work, bytes_accessed=4 * wide * width, transcendentals=0),
        name="meat_other",
    )(*args)


def solution(mesh):
    placed = (P("cal", "gr"), P("gr"), P("cal"), P("cal"), P("cal"), P("cal"), P())
    return jax.shard_map(
        per_device, mesh=mesh, in_specs=placed, out_specs=P("cal", "gr"), check_vma=False
    )
```

```python
import functools

import jax
import jax.numpy as jnp
from jax import lax
from jax.experimental import pallas as pl
from jax.experimental.pallas import tpu as pltpu
from jax.sharding import PartitionSpec as P

CL_DEV = 16
AXES = ("cal", "gr")
VMEM = pl.BlockSpec(memory_space=pltpu.VMEM)
SMEM = pl.BlockSpec(memory_space=pltpu.SMEM)
ANY = pl.BlockSpec(memory_space=pl.ANY)
LIMIT = 24 * 1024 * 1024


def position():
    fan = lax.axis_size("cal") // lax.axis_size("gr")
    cal, gr = lax.axis_index("cal"), lax.axis_index("gr")
    return cal, cal // fan, cal % fan, gr


def top_half():
    fan = lax.axis_size("cal") // lax.axis_size("gr")
    return position()[2] // (fan // 2)


def split_two(value):
    high = value.astype(jnp.bfloat16)
    low = (value - high.astype(jnp.float32)).astype(jnp.bfloat16)
    return high, low


def linear_kernel(feats, coef, lin, held, weights, sems):
    rows, width = held.shape
    step = min(512, rows)
    fetch = pltpu.make_async_copy(coef, weights, sems.at[rows // step])
    fetch.start()
    copies = []
    for i in range(0, rows, step):
        part = pl.ds(i, step)
        copies.append(pltpu.make_async_copy(feats.at[part], held.at[part], sems.at[i // step]))
        copies[-1].start()
    fetch.wait()
    scale = weights[...].reshape(1, width).astype(jnp.float32)
    for i in range(0, rows, step):
        copies[i // step].wait()
        total = jnp.zeros((step, 128), jnp.float32)
        for j in range(0, width, 128):
            total = total + held[i : i + step, j : j + 128].astype(jnp.float32) * scale[:, j : j + 128]
        lin[:, i : i + step] = jnp.sum(total.T, axis=0, keepdims=True)


def spread(total, outs):
    size = outs[0].shape[0]
    for k, out in enumerate(outs):
        out[...] = total[k * size : (k + 1) * size]


def picks_kernel(per_dev, group, terms, effect, *refs):
    exposure, claims, ids, period, held, *far, picks = refs[terms:]
    cal, high, _, _ = position()
    base = cal * per_dev
    shift = jnp.zeros(claims.shape, jnp.float32)
    effects = effect[...].reshape(1, effect.shape[0])
    place = lax.broadcasted_iota(jnp.int32, effects.shape, 1)
    for k in range(per_dev):
        value = jnp.sum(jnp.where(place == base + k, effects, 0.0), axis=1, keepdims=True)
        shift = jnp.where(period[...] == base + k, value, shift)
    sums = [ref[...] for ref in refs[:terms]]
    while len(sums) > 1:
        sums = [a + b for a, b in zip(sums[::2], sums[1::2])]
    linear = sums[0]
    resid = claims[...] - jnp.exp(linear + exposure[...] + shift)
    resid = resid.astype(jnp.bfloat16).astype(jnp.float32)
    clusters, rows = picks.shape
    for k in range(clusters // group):
        first = (high ^ k) * group
        cluster = lax.broadcasted_iota(jnp.int32, (group, rows), 0) + first
        picks[k * group : (k + 1) * group, :] = jnp.where(cluster == ids[...], resid, 0.0).astype(jnp.bfloat16)
    half, deep = far[0].shape[1], clusters // 2
    columns = pl.ds(pl.multiple_of((1 - top_half()) * half, half), half)
    spread(jnp.dot(picks[deep:, :], held[:, columns], preferred_element_type=jnp.float32), far)


def rest_kernel(picks, held, *outs):
    half, group = outs[0].shape[1], outs[0].shape[0]
    deep = picks.shape[0] // 2
    columns = pl.ds(pl.multiple_of((1 - top_half()) * half, half), half)
    spread(jnp.dot(picks[:deep, :], held[:, columns], preferred_element_type=jnp.float32), outs[: deep // group])
    columns = pl.ds(pl.multiple_of(top_half() * half, half), half)
    spread(jnp.dot(picks[...], held[:, columns], preferred_element_type=jnp.float32), outs[deep // group :])


def meat_columns(scale, left, parts, store):
    high, low = split_two(jnp.concatenate([p[...] for p in parts], axis=0))
    deep = jnp.concatenate([high, high], axis=0)
    left_high = left[: left.shape[0] // 2]
    dims = (((0,), (0,)), ((), ()))
    half = high.shape[1]
    block = min(256, half)
    for n in range(half // block):
        part = slice(n * block, (n + 1) * block)
        total = lax.dot_general(
            left, deep[:, part], dims, preferred_element_type=jnp.float32
        ) + lax.dot_general(left_high, low[:, part], dims, preferred_element_type=jnp.float32)
        store(n, total * scale)


def own_kernel(scale, have, *refs):
    refs, (out, left) = refs[:-2], refs[-2:]
    got, own = refs[:-2], refs[-2:]
    _, high, _, gr = position()
    rows = jnp.where((gr ^ high) % 2 == 0, have[...], jnp.concatenate([ref[...] for ref in got], axis=0))
    both = jnp.concatenate(split_two(rows), axis=0)
    left[...] = both

    def store(n, value):
        out[n] = value

    meat_columns(scale, both, own, store)


def other_kernel(scale, first, left, *refs):
    other, (out, held, sems) = refs[:-3], refs[-3:]
    parts, _, block = held.shape
    copies = []

    def send(source, n, spot):
        columns = pl.ds(pl.multiple_of((spot * parts + n) * block, block), block)
        copies.append(pltpu.make_async_copy(source.at[n], out.at[:, columns], sems.at[len(copies)]))
        copies[-1].start()

    def store(n, value):
        held[n] = value
        send(held, n, 1 - top_half())

    for n in range(parts):
        send(first, n, top_half())
    meat_columns(scale, left[...], other, store)
    for copy in copies:
        copy.wait()


def exchange(value, cal_bits, gr_bits, n_cal, n_gr):
    pairs = [
        (c * n_gr + g, (c ^ cal_bits) * n_gr + (g ^ gr_bits))
        for c in range(n_cal)
        for g in range(n_gr)
    ]
    return lax.ppermute(value, AXES, pairs)


def per_device(features, coef, log_exposure, claims, cluster_id, period, period_effect):
    rows, width = features.shape
    n_cal, n_gr = lax.axis_size("cal"), lax.axis_size("gr")
    clusters = CL_DEV * n_cal
    per_dev = period_effect.shape[0] // n_cal
    fan = n_cal // n_gr
    cal, gr = lax.axis_index("cal"), lax.axis_index("gr")
    high, low = cal // fan, cal % fan
    swap = functools.partial(exchange, n_cal=n_cal, n_gr=n_gr)

    def kernel(body, out_shape, args, scalars, name, flops=0, alias={}):
        outs = out_shape if isinstance(out_shape, tuple) else (out_shape,)
        call = pl.pallas_call(
            body,
            out_shape=out_shape,
            in_specs=[SMEM] * scalars + [VMEM] * (len(args) - scalars),
            out_specs=tuple(VMEM for _ in outs) if isinstance(out_shape, tuple) else VMEM,
            compiler_params=pltpu.CompilerParams(vmem_limit_bytes=LIMIT),
            cost_estimate=pl.CostEstimate(flops=flops, bytes_accessed=flops // 256, transcendentals=0),
            name=name,
            input_output_aliases=alias,
        )
        return call(*args)

    f32, bf16 = jnp.float32, jnp.bfloat16
    pieces = rows // min(512, rows)
    lin, features = pl.pallas_call(
        linear_kernel,
        out_shape=(jax.ShapeDtypeStruct((1, rows), f32), jax.ShapeDtypeStruct((rows, width), bf16)),
        in_specs=[ANY, ANY],
        out_specs=(VMEM, VMEM),
        scratch_shapes=[pltpu.VMEM((width,), bf16), pltpu.SemaphoreType.DMA((pieces + 1,))],
        compiler_params=pltpu.CompilerParams(vmem_limit_bytes=LIMIT),
        cost_estimate=pl.CostEstimate(flops=2 * rows * width, bytes_accessed=2 * rows * width, transcendentals=0),
        name="linear",
    )(*(pltpu.with_memory_space_constraint(value, pltpu.HBM) for value in (features, coef)))
    linears = [lin] + [swap(lin, 0, k) for k in [*range(n_gr // 2, n_gr), *range(1, n_gr // 2)]]

    half = width // 2
    deep = clusters // 2
    group = clusters // n_gr
    flat = [v.reshape(1, rows) for v in (log_exposure, claims, cluster_id, period)]
    work = 2 * rows * deep * half
    score = jax.ShapeDtypeStruct((group, half), f32)
    *far, picks = kernel(
        functools.partial(picks_kernel, per_dev, group, n_gr),
        (score,) * (n_gr // 2) + (jax.ShapeDtypeStruct((clusters, rows), bf16),),
        (period_effect, *linears, *flat, features),
        0, "send_far", work,
    )
    far = [swap(value, fan // 2, 0) for value in far]
    rest = kernel(rest_kernel, (score,) * (n_gr // 2 + n_gr), (picks, features), 0, "rest", 3 * work)
    there = [swap(value, fan // 2, 0) for value in rest[: n_gr // 2]] + far
    kept = rest[n_gr // 2 :]
    parts = []
    for k in range(n_gr):
        part = kept[k] + there[k]
        bits = fan // 4
        while bits:
            size = part.shape[1] // 2
            mine = (low // bits) % 2
            away = lax.dynamic_slice_in_dim(part, (1 - mine) * size, size, axis=1)
            part = lax.dynamic_slice_in_dim(part, mine * size, size, axis=1) + swap(away, bits, 0)
            bits //= 2
        parts.append(part)

    arrived = {k: swap(parts[k], k * fan, 0) for k in range(n_gr - 1, 0, -1)}
    owned = lax.optimization_barrier(arrived[n_gr // 2] + arrived[n_gr // 2 + 1])
    for k in [*range(n_gr // 2 + 2, n_gr), *range(1, n_gr // 2)]:
        owned = owned + arrived[k]
    owned = owned + parts[0]
    def along(value, k):
        table = [[2, 0, 3, 1], [1, 3, 0, 2], [3, 2, 1, 0]][k]
        pairs = []
        for c in range(n_cal):
            there = (table[c // fan] if n_gr == 4 else (c // fan) ^ (k + 1)) * fan + c % fan
            pairs += [(c * n_gr + g, there * n_gr + g) for g in range(n_gr)]
        return lax.ppermute(value, AXES, pairs)

    gathered = [owned] + [along(owned, k) for k in range(n_gr - 1)]
    blocks = [jnp.concatenate(gathered[0:2], axis=0), jnp.concatenate(gathered[2:4], axis=0)]
    sides, others = [], []
    for side in blocks:
        bits = 1
        while bits < fan // 2:
            mine = (low // bits) % 2
            away = swap(side, bits, 0)
            side = jnp.where(
                mine == 0, jnp.concatenate([side, away], axis=1), jnp.concatenate([away, side], axis=1)
            )
            bits *= 2
        sides.append(side)
        others.append(swap(side, fan // 2, 0))

    have = jnp.concatenate(gathered, axis=0)
    turn = gr ^ high
    bits = n_gr // 2
    while bits > 1:
        pairs = []
        for c in range(n_cal):
            for g in range(n_gr):
                step = (g ^ (c // fan)) & (2 * bits - 1)
                flip = bits if step == 0 or step == 2 * bits - 1 else bits // 2
                pairs.append((c * n_gr + g, c * n_gr + (g ^ flip)))
        if bits > 2:
            pairs = [(c * n_gr + g, c * n_gr + (g ^ bits)) for c in range(n_cal) for g in range(n_gr)]
        edges = [clusters * k // 16 for k in [0, 8, 12, 16]]
        got = jnp.concatenate([lax.ppermute(have[i:j], AXES, pairs) for i, j in zip(edges, edges[1:])], axis=0)
        got, *others[:1] = lax.optimization_barrier((got, *others[:1]))
        have = jnp.where((turn & bits) != 0, got, have)
        bits //= 2
    edges = [clusters * k // 16 for k in [0, 6, 12, 16]]
    got = [swap(have[i:j], 0, 1) for i, j in zip(edges, edges[1:])]
    scale = 1.0 / (rows * n_cal)
    wide, block = have.shape[1], min(256, half)
    parts = half // block
    work = 6 * clusters * half * wide
    first, left = kernel(
        functools.partial(own_kernel, scale),
        (jax.ShapeDtypeStruct((parts, wide, block), f32), jax.ShapeDtypeStruct((2 * clusters, wide), bf16)),
        (have, *got, *sides), 0, "meat_own",
    )
    args = (first, left, *others)
    return pl.pallas_call(
        functools.partial(other_kernel, scale),
        out_shape=jax.ShapeDtypeStruct((wide, width), f32),
        in_specs=[VMEM] * len(args),
        out_specs=ANY,
        scratch_shapes=[pltpu.VMEM((parts, wide, block), f32), pltpu.SemaphoreType.DMA((2 * parts,))],
        compiler_params=pltpu.CompilerParams(vmem_limit_bytes=LIMIT),
        cost_estimate=pl.CostEstimate(flops=work, bytes_accessed=4 * wide * width, transcendentals=0),
        name="meat_other",
    )(*args)


def solution(mesh):
    placed = (P("cal", "gr"), P("gr"), P("cal"), P("cal"), P("cal"), P("cal"), P())
    return jax.shard_map(
        per_device, mesh=mesh, in_specs=placed, out_specs=P("cal", "gr"), check_vma=False
    )
```

```python
import functools

import jax
import jax.numpy as jnp
from jax import lax
from jax.experimental import pallas as pl
from jax.experimental.pallas import tpu as pltpu
from jax.sharding import PartitionSpec as P

CL_DEV = 16
AXES = ("cal", "gr")
VMEM = pl.BlockSpec(memory_space=pltpu.VMEM)
SMEM = pl.BlockSpec(memory_space=pltpu.SMEM)
ANY = pl.BlockSpec(memory_space=pl.ANY)
LIMIT = 24 * 1024 * 1024


def position():
    fan = lax.axis_size("cal") // lax.axis_size("gr")
    cal, gr = lax.axis_index("cal"), lax.axis_index("gr")
    return cal, cal // fan, cal % fan, gr


def top_half():
    fan = lax.axis_size("cal") // lax.axis_size("gr")
    return position()[2] // (fan // 2)


def split_two(value):
    high = value.astype(jnp.bfloat16)
    low = (value - high.astype(jnp.float32)).astype(jnp.bfloat16)
    return high, low


def linear_kernel(feats, coef, lin, held, weights, sems):
    rows, width = held.shape
    step = min(512, rows)
    fetch = pltpu.make_async_copy(coef, weights, sems.at[rows // step])
    fetch.start()
    copies = []
    for i in range(0, rows, step):
        part = pl.ds(i, step)
        copies.append(pltpu.make_async_copy(feats.at[part], held.at[part], sems.at[i // step]))
        copies[-1].start()
    fetch.wait()
    scale = weights[...].reshape(1, width).astype(jnp.float32)
    for i in range(0, rows, step):
        copies[i // step].wait()
        total = jnp.zeros((step, 128), jnp.float32)
        for j in range(0, width, 128):
            total = total + held[i : i + step, j : j + 128].astype(jnp.float32) * scale[:, j : j + 128]
        lin[:, i : i + step] = jnp.sum(total.T, axis=0, keepdims=True)


def spread(total, outs):
    size = outs[0].shape[0]
    for k, out in enumerate(outs):
        out[...] = total[k * size : (k + 1) * size]


def picks_kernel(per_dev, group, terms, effect, *refs):
    exposure, claims, ids, period, held, *far, picks = refs[terms:]
    cal, high, _, _ = position()
    base = cal * per_dev
    shift = jnp.zeros(claims.shape, jnp.float32)
    effects = effect[...].reshape(1, effect.shape[0])
    place = lax.broadcasted_iota(jnp.int32, effects.shape, 1)
    for k in range(per_dev):
        value = jnp.sum(jnp.where(place == base + k, effects, 0.0), axis=1, keepdims=True)
        shift = jnp.where(period[...] == base + k, value, shift)
    sums = [ref[...] for ref in refs[:terms]]
    while len(sums) > 1:
        sums = [a + b for a, b in zip(sums[::2], sums[1::2])]
    linear = sums[0]
    resid = claims[...] - jnp.exp(linear + exposure[...] + shift)
    resid = resid.astype(jnp.bfloat16).astype(jnp.float32)
    clusters, rows = picks.shape
    for k in range(clusters // group):
        first = (high ^ k) * group
        cluster = lax.broadcasted_iota(jnp.int32, (group, rows), 0) + first
        picks[k * group : (k + 1) * group, :] = jnp.where(cluster == ids[...], resid, 0.0).astype(jnp.bfloat16)
    half, deep = far[0].shape[1], clusters // 2
    columns = pl.ds(pl.multiple_of((1 - top_half()) * half, half), half)
    spread(jnp.dot(picks[deep:, :], held[:, columns], preferred_element_type=jnp.float32), far)


def rest_kernel(picks, held, *outs):
    half, group = outs[0].shape[1], outs[0].shape[0]
    deep = picks.shape[0] // 2
    columns = pl.ds(pl.multiple_of((1 - top_half()) * half, half), half)
    spread(jnp.dot(picks[:deep, :], held[:, columns], preferred_element_type=jnp.float32), outs[: deep // group])
    columns = pl.ds(pl.multiple_of(top_half() * half, half), half)
    spread(jnp.dot(picks[...], held[:, columns], preferred_element_type=jnp.float32), outs[deep // group :])


def meat_columns(scale, left, parts, store):
    high, low = split_two(jnp.concatenate([p[...] for p in parts], axis=0))
    deep = jnp.concatenate([high, high], axis=0)
    left_high = left[: left.shape[0] // 2]
    dims = (((0,), (0,)), ((), ()))
    half = high.shape[1]
    block = min(512, half)
    for n in range(half // block):
        part = slice(n * block, (n + 1) * block)
        total = lax.dot_general(
            left, deep[:, part], dims, preferred_element_type=jnp.float32
        ) + lax.dot_general(left_high, low[:, part], dims, preferred_element_type=jnp.float32)
        store(n, total * scale)


def own_kernel(scale, have, *refs):
    refs, (out, left) = refs[:-2], refs[-2:]
    got, own = refs[:-2], refs[-2:]
    _, high, _, gr = position()
    rows = jnp.where((gr ^ high) % 2 == 0, have[...], jnp.concatenate([ref[...] for ref in got], axis=0))
    both = jnp.concatenate(split_two(rows), axis=0)
    left[...] = both

    def store(n, value):
        out[n] = value

    meat_columns(scale, both, own, store)


def other_kernel(scale, first, left, *refs):
    other, (out, held, sems) = refs[:-3], refs[-3:]
    parts, _, block = held.shape
    copies = []

    def send(source, n, spot):
        columns = pl.ds(pl.multiple_of((spot * parts + n) * block, block), block)
        copies.append(pltpu.make_async_copy(source.at[n], out.at[:, columns], sems.at[len(copies)]))
        copies[-1].start()

    def store(n, value):
        held[n] = value
        send(held, n, 1 - top_half())

    for n in range(parts):
        send(first, n, top_half())
    meat_columns(scale, left[...], other, store)
    for copy in copies:
        copy.wait()


def exchange(value, cal_bits, gr_bits, n_cal, n_gr):
    pairs = [
        (c * n_gr + g, (c ^ cal_bits) * n_gr + (g ^ gr_bits))
        for c in range(n_cal)
        for g in range(n_gr)
    ]
    return lax.ppermute(value, AXES, pairs)


def per_device(features, coef, log_exposure, claims, cluster_id, period, period_effect):
    rows, width = features.shape
    n_cal, n_gr = lax.axis_size("cal"), lax.axis_size("gr")
    clusters = CL_DEV * n_cal
    per_dev = period_effect.shape[0] // n_cal
    fan = n_cal // n_gr
    cal, gr = lax.axis_index("cal"), lax.axis_index("gr")
    high, low = cal // fan, cal % fan
    swap = functools.partial(exchange, n_cal=n_cal, n_gr=n_gr)

    def kernel(body, out_shape, args, scalars, name, flops=0, alias={}):
        outs = out_shape if isinstance(out_shape, tuple) else (out_shape,)
        call = pl.pallas_call(
            body,
            out_shape=out_shape,
            in_specs=[SMEM] * scalars + [VMEM] * (len(args) - scalars),
            out_specs=tuple(VMEM for _ in outs) if isinstance(out_shape, tuple) else VMEM,
            compiler_params=pltpu.CompilerParams(vmem_limit_bytes=LIMIT),
            cost_estimate=pl.CostEstimate(flops=flops, bytes_accessed=flops // 256, transcendentals=0),
            name=name,
            input_output_aliases=alias,
        )
        return call(*args)

    f32, bf16 = jnp.float32, jnp.bfloat16
    pieces = rows // min(512, rows)
    lin, features = pl.pallas_call(
        linear_kernel,
        out_shape=(jax.ShapeDtypeStruct((1, rows), f32), jax.ShapeDtypeStruct((rows, width), bf16)),
        in_specs=[ANY, ANY],
        out_specs=(VMEM, VMEM),
        scratch_shapes=[pltpu.VMEM((width,), bf16), pltpu.SemaphoreType.DMA((pieces + 1,))],
        compiler_params=pltpu.CompilerParams(vmem_limit_bytes=LIMIT),
        cost_estimate=pl.CostEstimate(flops=2 * rows * width, bytes_accessed=2 * rows * width, transcendentals=0),
        name="linear",
    )(*(pltpu.with_memory_space_constraint(value, pltpu.HBM) for value in (features, coef)))
    linears = [lin] + [swap(lin, 0, k) for k in [*range(n_gr // 2, n_gr), *range(1, n_gr // 2)]]

    half = width // 2
    deep = clusters // 2
    group = clusters // n_gr
    flat = [v.reshape(1, rows) for v in (log_exposure, claims, cluster_id, period)]
    work = 2 * rows * deep * half
    score = jax.ShapeDtypeStruct((group, half), f32)
    *far, picks = kernel(
        functools.partial(picks_kernel, per_dev, group, n_gr),
        (score,) * (n_gr // 2) + (jax.ShapeDtypeStruct((clusters, rows), bf16),),
        (period_effect, *linears, *flat, features),
        0, "send_far", work,
    )
    far = [swap(value, fan // 2, 0) for value in far]
    rest = kernel(rest_kernel, (score,) * (n_gr // 2 + n_gr), (picks, features), 0, "rest", 3 * work)
    there = [swap(value, fan // 2, 0) for value in rest[: n_gr // 2]] + far
    kept = rest[n_gr // 2 :]
    parts = []
    for k in range(n_gr):
        part = kept[k] + there[k]
        bits = fan // 4
        while bits:
            size = part.shape[1] // 2
            mine = (low // bits) % 2
            away = lax.dynamic_slice_in_dim(part, (1 - mine) * size, size, axis=1)
            part = lax.dynamic_slice_in_dim(part, mine * size, size, axis=1) + swap(away, bits, 0)
            bits //= 2
        parts.append(part)

    arrived = {k: swap(parts[k], k * fan, 0) for k in range(n_gr - 1, 0, -1)}
    owned = lax.optimization_barrier(arrived[n_gr // 2] + arrived[n_gr // 2 + 1])
    for k in [*range(n_gr // 2 + 2, n_gr), *range(1, n_gr // 2)]:
        owned = owned + arrived[k]
    owned = owned + parts[0]
    def along(value, k):
        table = [[2, 0, 3, 1], [1, 3, 0, 2], [3, 2, 1, 0]][k]
        pairs = []
        for c in range(n_cal):
            there = (table[c // fan] if n_gr == 4 else (c // fan) ^ (k + 1)) * fan + c % fan
            pairs += [(c * n_gr + g, there * n_gr + g) for g in range(n_gr)]
        return lax.ppermute(value, AXES, pairs)

    gathered = [owned] + [along(owned, k) for k in range(n_gr - 1)]
    blocks = [jnp.concatenate(gathered[0:2], axis=0), jnp.concatenate(gathered[2:4], axis=0)]
    sides, others = [], []
    for side in blocks:
        bits = 1
        while bits < fan // 2:
            mine = (low // bits) % 2
            away = swap(side, bits, 0)
            side = jnp.where(
                mine == 0, jnp.concatenate([side, away], axis=1), jnp.concatenate([away, side], axis=1)
            )
            bits *= 2
        sides.append(side)
        others.append(swap(side, fan // 2, 0))

    have = jnp.concatenate(gathered, axis=0)
    turn = gr ^ high
    bits = n_gr // 2
    while bits > 1:
        pairs = []
        for c in range(n_cal):
            for g in range(n_gr):
                step = (g ^ (c // fan)) & (2 * bits - 1)
                flip = bits if step == 0 or step == 2 * bits - 1 else bits // 2
                pairs.append((c * n_gr + g, c * n_gr + (g ^ flip)))
        if bits > 2:
            pairs = [(c * n_gr + g, c * n_gr + (g ^ bits)) for c in range(n_cal) for g in range(n_gr)]
        edges = [clusters * k // 16 for k in [0, 8, 12, 16]]
        got = jnp.concatenate([lax.ppermute(have[i:j], AXES, pairs) for i, j in zip(edges, edges[1:])], axis=0)
        got, *others[:1] = lax.optimization_barrier((got, *others[:1]))
        have = jnp.where((turn & bits) != 0, got, have)
        bits //= 2
    edges = [clusters * k // 16 for k in [0, 6, 12, 16]]
    got = [swap(have[i:j], 0, 1) for i, j in zip(edges, edges[1:])]
    scale = 1.0 / (rows * n_cal)
    wide, block = have.shape[1], min(512, half)
    parts = half // block
    work = 6 * clusters * half * wide
    first, left = kernel(
        functools.partial(own_kernel, scale),
        (jax.ShapeDtypeStruct((parts, wide, block), f32), jax.ShapeDtypeStruct((2 * clusters, wide), bf16)),
        (have, *got, *sides), 0, "meat_own",
    )
    args = (first, left, *others)
    return pl.pallas_call(
        functools.partial(other_kernel, scale),
        out_shape=jax.ShapeDtypeStruct((wide, width), f32),
        in_specs=[VMEM] * len(args),
        out_specs=ANY,
        scratch_shapes=[pltpu.VMEM((parts, wide, block), f32), pltpu.SemaphoreType.DMA((2 * parts,))],
        compiler_params=pltpu.CompilerParams(vmem_limit_bytes=LIMIT),
        cost_estimate=pl.CostEstimate(flops=work, bytes_accessed=4 * wide * width, transcendentals=0),
        name="meat_other",
    )(*args)


def solution(mesh):
    placed = (P("cal", "gr"), P("gr"), P("cal"), P("cal"), P("cal"), P("cal"), P())
    return jax.shard_map(
        per_device, mesh=mesh, in_specs=placed, out_specs=P("cal", "gr"), check_vma=False
    )
```
